32 devices in a mesh: pipe: 16 (over z, y, core), ctx: 2 (over x).
Axes of the slice: x: 2, y: 2, z: 4, core: 2. Of those that a mesh axis runs over, the one named last changes fastest.
Arguments:
- query: bfloat16 [16, 256, 8192], P('pipe', 'ctx'), may hold values from -6 to 6
- inner: bfloat16 [16, 256, 8192], P('pipe', 'ctx'), may hold values from -6 to 6
- out_grad: bfloat16 [16, 256, 8192], P('pipe', 'ctx'), may hold values from -6 to 6
- filters: float32 [16, 7, 8192], P('pipe'), as said below
- trace_lengths: int32 [16, 2], P('pipe'), may hold values from 1 to 192, 256 in all within a row
Outputs:
- passed_grad: bfloat16 [2, 16, 256, 8192], P(None, 'pipe', 'ctx')
- filter_grad: float32 [16, 7, 8192], P('pipe', None, 'ctx')
The draws below stay inside these ranges and needn't reach their ends.
Inputs may be any that keep to these rules, and one draw needn't show every extreme that they name: filters of section s and section 15 - s are equal (the same layer).
All inputs are finite; a program needn't handle non-finite values.
Results may differ from the reference program's by a relative error of at most 0.0041.
Values may be sent and summed in bfloat16 or wider, within the bound.
A program may use at most 128 MiB of HBM per device.

```python
import math
import jax
import jax.numpy as jnp
import numpy as np
from jax import lax

D = 8192
K = 7
NSEG = 2
TOK_DEV = 128
TOKENS = 256
N_PIPE = 16


def draw_filters(key, part):
    half = jnp.clip(jax.random.normal(key, (N_PIPE // 2, K, D), jnp.float32) * 0.4, -1.6, 1.6)
    return jnp.concatenate([half, half[::-1]], axis=0)


def levels(stream_key, shape, shards, smallest, top_value):
    gain, own = 1.0, jax.random.fold_in(stream_key, 6)
    for dim, shards_of in shards:
        draws = jnp.exp(jax.random.uniform(jax.random.fold_in(own, dim), (shards_of,), jnp.float32, smallest / len(shards), top_value / len(shards)))
        gain = gain * jnp.repeat(draws, shape[dim] // shards_of).reshape([-1 if axis == dim else 1 for axis in range(len(shape))])
    return gain


def profile(count, total, bound, skew):
    weights = [(1 << 20) // math.isqrt(grade ** skew) + 1 for grade in range(2, count + 1)]
    surplus, holding = total - bound - (count - 1), [1] * (count - 1)
    while surplus > 0:
        movable = [i for i in range(count - 1) if holding[i] < bound]
        pool, remaining = sum([weights[i] for i in movable]), surplus
        for i in movable:
            extra = min(bound - holding[i], max(1, remaining * weights[i] // pool), surplus)
            holding[i] = holding[i] + extra
            surplus = surplus - extra
    return np.array([bound] + holding)


def ragged(rng, amount, total, limit, lean):
    if amount == 2:
        one = jax.random.randint(rng, (), max(1, total - limit), min(limit, total - 1) + 1)
        return jnp.stack([one, total - one])
    tallies = jnp.asarray(profile(amount, total, limit, lean), jnp.int32)
    couples = (amount - 1) // 2
    giver, sink = tallies[1:1 + 2 * couples:2], tallies[2:2 + 2 * couples:2]
    slack = jnp.minimum(giver - 1, limit - sink)
    shifted = jax.random.randint(jax.random.fold_in(rng, 1), (couples,), 0, 1 << 20) % (slack + 1)
    tallies = tallies.at[1:1 + 2 * couples:2].set(giver - shifted).at[2:2 + 2 * couples:2].set(sink + shifted)
    return tallies[jax.random.permutation(jax.random.fold_in(rng, 2), amount)]


def noise(stream_key, dims, deviation, most, cuts=(), kind=jnp.bfloat16):
    values = jax.random.normal(stream_key, dims, jnp.float32) * deviation
    if len(cuts) > 0:
        values = levels(stream_key, dims, cuts, -0.22, 0.18) * values
    return jnp.clip(values, min=-most, max=most).astype(kind)


def setup_inputs(seed: int = 0) -> dict:
    keys = jax.random.split(jax.random.key(seed), 6)
    return {
        "query": noise(keys[0], (N_PIPE, TOKENS, D), 1.0, 6.0, ((0, 16), (1, 2))),
        "inner": noise(keys[1], (N_PIPE, TOKENS, D), 1.0, 6.0, ((0, 16), (1, 2))),
        "out_grad": noise(keys[2], (N_PIPE, TOKENS, D), 1.0, 6.0, ((0, 16), (1, 2))),
        "filters": draw_filters(jax.random.fold_in(keys[5], 71), 0),
        "trace_lengths": jax.vmap(lambda own: ragged(own, NSEG, TOKENS, TOKENS - TOK_DEV // 2, 0))(jax.random.split(keys[4], N_PIPE)).reshape((N_PIPE, NSEG)).astype(jnp.int32),
    }


def seg_of(pos, ends):
    return jnp.sum((pos[:, None] >= ends[None, :]).astype(jnp.int32), axis=1)


def section_grads(items):
    query, inner, out_grad, filters, lengths = items
    ends = jnp.cumsum(lengths).astype(jnp.int32)
    pos = jnp.arange(TOKENS, dtype=jnp.int32)
    seg = seg_of(pos, ends)
    inner_f = inner.astype(jnp.float32)
    out_f = out_grad.astype(jnp.float32)
    gz = (out_f * query.astype(jnp.float32)).astype(jnp.bfloat16)
    gz_f = gz.astype(jnp.float32)
    zsum = jnp.zeros((TOKENS, D), jnp.float32)
    usum = jnp.zeros((TOKENS, D), jnp.float32)
    taps = []
    for j in range(K):
        back_u = jnp.concatenate([jnp.zeros((j, D), jnp.float32), inner_f[:TOKENS - j]], axis=0)
        back_seg = seg_of(pos - j, ends)
        mask_b = (seg == back_seg).astype(jnp.float32)[:, None]
        zsum = zsum + filters[j][None, :] * back_u * mask_b
        taps.append(jnp.sum(gz_f * back_u * mask_b, axis=0))
        ahead_g = jnp.concatenate([gz_f[j:], jnp.zeros((j, D), jnp.float32)], axis=0)
        ahead_seg = seg_of(pos + j, ends)
        mask_a = (seg == ahead_seg).astype(jnp.float32)[:, None]
        usum = usum + filters[j][None, :] * ahead_g * mask_a
    grad_q = (out_f * zsum).astype(jnp.bfloat16)
    grad_u = usum.astype(jnp.bfloat16)
    return grad_q, grad_u, jnp.stack(taps)


def reference(query, inner, out_grad, filters, trace_lengths):
    grad_q, grad_u, taps = lax.map(section_grads, (query, inner, out_grad, filters, trace_lengths))
    filter_grad = taps + taps[::-1]
    both = jnp.stack([grad_q, grad_u])
    tail = jnp.zeros((2, 1, TOKENS, D), jnp.bfloat16)
    passed_grad = jnp.concatenate([both[:, 1:], tail], axis=1)
    return passed_grad, filter_grad
```

```python
import functools

import jax
import jax.numpy as jnp
from jax import lax
from jax.experimental import pallas as pl
from jax.experimental.pallas import tpu as pltpu
from jax.sharding import PartitionSpec as P

MESH = pl.DeviceIdType.MESH
EDGE = 16
LANES = 128
CHUNK = 512


def fold(x):
    return x[: EDGE // 2] + x[EDGE // 2 :]


def rounded_product(a, b):
    return (a.astype(jnp.float32) * b.astype(jnp.float32)).astype(jnp.bfloat16).astype(jnp.float32)


def kernel(
    n_pipe, n_ctx, n_seg,
    lengths, query, inner, out_grad, filters, arrived, summed,
    q_v, u_v, g_v, f_v, u_left, q_right, g_right, u_f, gz_f, masks, parts, staged, dh, dh_in, total, mirrored,
    load_sem, filter_sem, halo_send, halo_recv, out_send, out_recv, edge_send, edge_recv, dh_send, dh_recv, mirror_send, mirror_recv,
):
    taps, _, width = filters.shape
    rows = query.shape[0]
    own = width // n_ctx
    chunks = width // CHUNK
    s = lax.axis_index("pipe")
    c = lax.axis_index("ctx")
    first, last = s == 0, s == n_pipe - 1
    before, after = lax.rem(s + n_pipe - 1, n_pipe), lax.rem(s + 1, n_pipe)
    mirror = n_pipe - 1 - s

    def cols_of(i):
        return pl.ds(pl.multiple_of(i * CHUNK, CHUNK), CHUNK)

    def loads(i):
        cols = cols_of(i)
        return [
            pltpu.make_async_copy(src.at[:, cols], dst.at[:, cols], load_sem.at[k, i])
            for k, (src, dst) in enumerate(((query, q_v), (inner, u_v), (out_grad, g_v)))
        ]

    filter_load = pltpu.make_async_copy(filters, f_v, filter_sem)
    filter_load.start()
    for i in range(2):
        for load in loads(i):
            load.start()

    barrier = pltpu.get_barrier_semaphore()
    for other in (before, after, mirror):
        pl.semaphore_signal(barrier, inc=1, device_id={"pipe": other}, device_id_type=MESH)
    for d in range(1, n_ctx):
        pl.semaphore_signal(barrier, inc=1, device_id={"ctx": lax.rem(c + d, n_ctx)}, device_id_type=MESH)

    ends = []
    for k in range(n_seg):
        ends.append(lengths[0, k] + (ends[-1] if ends else 0))
    pos = c * rows + lax.broadcasted_iota(jnp.int32, (rows + EDGE, LANES), 0)

    def seg_of(at):
        return sum((at >= end).astype(jnp.int32) for end in ends)

    seg = seg_of(pos)
    for j in range(1, taps):
        masks[j - 1] = (seg == seg_of(pos - j)).astype(jnp.float32)

    def back(j, base, mask_at):
        x = u_f[base - j : base - j + EDGE]
        return x if j == 0 else x * masks[j - 1, mask_at : mask_at + EDGE]

    def ahead(j, base, mask_at):
        x = gz_f[base + j : base + j + EDGE]
        return x if j == 0 else x * masks[j - 1, mask_at + j : mask_at + j + EDGE]

    def taps_at(cols):
        return [jnp.broadcast_to(f_v[j, :, cols], (EDGE, LANES)) for j in range(taps)]

    def interior(i):
        def group(l, carry):
            cols = pl.ds(pl.multiple_of(i * CHUNK + l * LANES, LANES), LANES)
            u_f[EDGE : EDGE + rows] = u_v[:, cols].astype(jnp.float32)
            gz_f[:rows] = rounded_product(g_v[:, cols], q_v[:, cols])
            f = taps_at(cols)
            sums = [jnp.zeros((EDGE // 2, LANES), jnp.float32)] * taps
            for at in range(0, rows, EDGE):
                if at > 0:
                    gz = gz_f[at : at + EDGE]
                    z = None
                    for j in range(taps):
                        u = back(j, EDGE + at, at)
                        z = f[j] * u if z is None else z + f[j] * u
                        sums[j] = sums[j] + fold(gz * u)
                    staged[0, at : at + EDGE, cols] = (g_v[at : at + EDGE, cols].astype(jnp.float32) * z).astype(jnp.bfloat16)
                if at < rows - EDGE:
                    z = f[0] * ahead(0, at, at)
                    for j in range(1, taps):
                        z = z + f[j] * ahead(j, at, at)
                    staged[1, at : at + EDGE, cols] = z.astype(jnp.bfloat16)
            for j in range(taps):
                parts[j, :, cols] = sums[j]
            return carry

        lax.fori_loop(0, CHUNK // LANES, group, 0)

    def edges(l, carry):
        cols = pl.ds(pl.multiple_of(l * LANES, LANES), LANES)
        f = taps_at(cols)
        u_f[:EDGE] = u_left[:, cols].astype(jnp.float32)
        u_f[EDGE : 2 * EDGE] = u_v[:EDGE, cols].astype(jnp.float32)
        gz_f[:EDGE] = rounded_product(g_v[rows - EDGE :, cols], q_v[rows - EDGE :, cols])
        gz_f[EDGE : 2 * EDGE] = rounded_product(g_right[:, cols], q_right[:, cols])
        gz = rounded_product(g_v[:EDGE, cols], q_v[:EDGE, cols])
        z = None
        for j in range(taps):
            u = back(j, EDGE, 0)
            z = f[j] * u if z is None else z + f[j] * u
            dh[j : j + 1, cols] = jnp.sum(parts[j, :, cols] + fold(gz * u), axis=0, keepdims=True)
        staged[0, :EDGE, cols] = (g_v[:EDGE, cols].astype(jnp.float32) * z).astype(jnp.bfloat16)
        z = f[0] * ahead(0, 0, rows - EDGE)
        for j in range(1, taps):
            z = z + f[j] * ahead(j, 0, rows - EDGE)
        staged[1, rows - EDGE :, cols] = z.astype(jnp.bfloat16)
        return carry

    def sends(i):
        cols = cols_of(i)
        return [
            pltpu.make_async_remote_copy(
                src_ref=staged.at[k, at, cols], dst_ref=arrived.at[k, 0, at, cols],
                send_sem=out_send.at[k, i], recv_sem=out_recv.at[k, i],
                device_id={"pipe": before}, device_id_type=MESH,
            )
            for k, at in enumerate((pl.ds(EDGE, rows - EDGE), pl.ds(0, rows - EDGE)))
        ]

    def edge_sends():
        return [
            pltpu.make_async_remote_copy(
                src_ref=staged.at[k, at], dst_ref=arrived.at[k, 0, at],
                send_sem=edge_send.at[k], recv_sem=edge_recv.at[k],
                device_id={"pipe": before}, device_id_type=MESH,
            )
            for k, at in enumerate((pl.ds(0, EDGE), pl.ds(rows - EDGE, EDGE)))
        ]

    def halo(k, src, dst, other):
        return pltpu.make_async_remote_copy(
            src_ref=src, dst_ref=dst, send_sem=halo_send.at[k], recv_sem=halo_recv.at[k],
            device_id={"ctx": other}, device_id_type=MESH,
        )

    to_right = [halo(0, inner.at[pl.ds(rows - EDGE, EDGE)], u_left, lax.rem(c + 1, n_ctx))]
    to_left = [
        halo(1, query.at[pl.ds(0, EDGE)], q_right, lax.rem(c + n_ctx - 1, n_ctx)),
        halo(2, out_grad.at[pl.ds(0, EDGE)], g_right, lax.rem(c + n_ctx - 1, n_ctx)),
    ]

    def step(i, carry):
        @pl.when(i + 2 < chunks)
        def _():
            for load in loads(i + 2):
                load.start()

        for load in loads(i):
            load.wait()
        interior(i)

        @pl.when(jnp.logical_not(first))
        def _():
            for send in sends(i):
                send.start()

        return carry

    filter_load.wait()
    for load in loads(2):
        load.start()
    for load in loads(0):
        load.wait()
    interior(0)
    pl.semaphore_wait(barrier, 3 + n_ctx - 1)

    @pl.when(jnp.logical_not(first))
    def _():
        for send in sends(0):
            send.start()

    @pl.when(c < n_ctx - 1)
    def _():
        for send in to_right:
            send.start()

    @pl.when(c > 0)
    def _():
        for send in to_left:
            send.start()

    @pl.when(c == 0)
    def _():
        u_left[...] = jnp.zeros_like(u_left)

    @pl.when(c == n_ctx - 1)
    def _():
        q_right[...] = jnp.zeros_like(q_right)
        g_right[...] = jnp.zeros_like(g_right)

    lax.fori_loop(1, chunks, step, 0)

    @pl.when(c > 0)
    def _():
        for send in to_right:
            send.wait_recv()

    @pl.when(c < n_ctx - 1)
    def _():
        for send in to_left:
            send.wait_recv()

    dh[...] = jnp.zeros_like(dh)
    lax.fori_loop(0, width // LANES, edges, 0)

    @pl.when(jnp.logical_not(first))
    def _():
        for send in edge_sends():
            send.start()

    shares = []
    for d in range(1, n_ctx):
        other = lax.rem(c + d, n_ctx)
        shares.append(
            pltpu.make_async_remote_copy(
                src_ref=dh.at[:, pl.ds(pl.multiple_of(other * own, own), own)], dst_ref=dh_in.at[d - 1],
                send_sem=dh_send.at[d - 1], recv_sem=dh_recv.at[d - 1],
                device_id={"ctx": other}, device_id_type=MESH,
            )
        )
    for share in shares:
        share.start()
    for share in shares:
        share.wait_recv()
    mine = dh[:, pl.ds(pl.multiple_of(c * own, own), own)]
    for d in range(1, n_ctx):
        mine = mine + dh_in[d - 1]
    total[...] = mine
    swap = pltpu.make_async_remote_copy(
        src_ref=total, dst_ref=mirrored, send_sem=mirror_send, recv_sem=mirror_recv,
        device_id={"pipe": mirror}, device_id_type=MESH,
    )
    swap.start()

    @pl.when(last)
    def _():
        arrived[...] = jnp.zeros_like(arrived)

    swap.wait_recv()
    summed[...] = total[...] + mirrored[...]
    swap.wait_send()
    for share in shares:
        share.wait_send()

    @pl.when(c < n_ctx - 1)
    def _():
        for send in to_right:
            send.wait_send()

    @pl.when(c > 0)
    def _():
        for send in to_left:
            send.wait_send()

    @pl.when(jnp.logical_not(first))
    def _():
        def drained(i, carry):
            for send in sends(i):
                send.wait_send()
            return carry

        lax.fori_loop(0, chunks, drained, 0)
        for send in edge_sends():
            send.wait_send()

    @pl.when(jnp.logical_not(last))
    def _():
        def landed(i, carry):
            for send in sends(i):
                send.wait_recv()
            return carry

        lax.fori_loop(0, chunks, landed, 0)
        for send in edge_sends():
            send.wait_recv()


def finish(arrived, summed, passed, grad, sem):
    copies = [pltpu.make_async_copy(arrived.at[k], passed.at[k], sem.at[k]) for k in range(2)]
    for copy in copies:
        copy.start()
    for j in range(grad.shape[0]):
        grad[j] = summed[j : j + 1]
    for copy in copies:
        copy.wait()


def local(n_pipe, n_ctx, query, inner, out_grad, filters, trace_lengths):
    _, rows, width = query.shape
    taps = filters.shape[1]
    own = width // n_ctx
    chunks = width // CHUNK
    anywhere = pl.BlockSpec(memory_space=pl.ANY)
    vmem = pl.BlockSpec(memory_space=pltpu.VMEM)
    f32, bf16, dma = jnp.float32, jnp.bfloat16, pltpu.SemaphoreType.DMA
    arrived, summed = pl.pallas_call(
        functools.partial(kernel, n_pipe, n_ctx, trace_lengths.shape[1]),
        out_shape=(pltpu.VMEM((2, 1, rows, width), bf16), pltpu.VMEM((8, own), f32)),
        in_specs=[pl.BlockSpec(memory_space=pltpu.SMEM)] + [anywhere] * 4,
        out_specs=(vmem, vmem),
        scratch_shapes=[
            pltpu.VMEM((rows, width), bf16),
            pltpu.VMEM((rows, width), bf16),
            pltpu.VMEM((rows, width), bf16),
            pltpu.VMEM((taps, 1, width), f32),
            pltpu.VMEM((EDGE, width), bf16),
            pltpu.VMEM((EDGE, width), bf16),
            pltpu.VMEM((EDGE, width), bf16),
            pltpu.VMEM((rows + EDGE, LANES), f32),
            pltpu.VMEM((rows + EDGE, LANES), f32),
            pltpu.VMEM((taps - 1, rows + EDGE, LANES), f32),
            pltpu.VMEM((taps, EDGE // 2, width), f32),
            pltpu.VMEM((2, rows, width), bf16),
            pltpu.VMEM((8, width), f32),
            pltpu.VMEM((n_ctx - 1, 8, own), f32),
            pltpu.VMEM((8, own), f32),
            pltpu.VMEM((8, own), f32),
            dma((3, chunks)),
            dma,
            dma((3,)),
            dma((3,)),
            dma((2, chunks)),
            dma((2, chunks)),
            dma((2,)),
            dma((2,)),
            dma((n_ctx - 1,)),
            dma((n_ctx - 1,)),
            dma,
            dma,
        ],
        compiler_params=pltpu.CompilerParams(collective_id=0, has_side_effects=True, vmem_limit_bytes=48 * 1024 * 1024),
        name="grads_passed_on",
    )(trace_lengths, query[0], inner[0], out_grad[0], jnp.swapaxes(filters, 0, 1))
    passed, grad = pl.pallas_call(
        finish,
        out_shape=(
            jax.ShapeDtypeStruct((2, 1, rows, width), bf16),
            jax.ShapeDtypeStruct((taps, 1, own), f32),
        ),
        in_specs=[anywhere, vmem],
        out_specs=(anywhere, vmem),
        scratch_shapes=[dma((2,))],
        name="results_written",
    )(arrived, summed)
    return passed, jnp.swapaxes(grad, 0, 1)


def solution(mesh):
    in_specs = (
        P("pipe", "ctx", None),
        P("pipe", "ctx", None),
        P("pipe", "ctx", None),
        P("pipe", None, None),
        P("pipe", None),
    )
    out_specs = (P(None, "pipe", "ctx", None), P("pipe", None, "ctx"))
    run = functools.partial(local, mesh.shape["pipe"], mesh.shape["ctx"])
    return jax.shard_map(run, mesh=mesh, in_specs=in_specs, out_specs=out_specs, check_vma=False)
```

```python
import functools

import jax
import jax.numpy as jnp
from jax import lax
from jax.experimental import pallas as pl
from jax.experimental.pallas import tpu as pltpu
from jax.sharding import PartitionSpec as P

MESH = pl.DeviceIdType.MESH
EDGE = 16
LANES = 128
CHUNK = 512


def fold(x):
    return x[: EDGE // 2] + x[EDGE // 2 :]


def rounded_product(a, b):
    return (a.astype(jnp.float32) * b.astype(jnp.float32)).astype(jnp.bfloat16).astype(jnp.float32)


def kernel(
    n_pipe, n_ctx, n_seg,
    lengths, query, inner, out_grad, filters, arrived, summed,
    q_v, u_v, g_v, f_v, u_left, q_right, g_right, u_f, gz_f, masks, parts, staged, dh, dh_in, total, mirrored,
    load_sem, filter_sem, halo_send, halo_recv, out_send, out_recv, edge_send, edge_recv, dh_send, dh_recv, mirror_send, mirror_recv,
):
    taps, _, width = filters.shape
    rows = query.shape[0]
    own = width // n_ctx
    chunks = width // CHUNK
    s = lax.axis_index("pipe")
    c = lax.axis_index("ctx")
    first, last = s == 0, s == n_pipe - 1
    before, after = lax.rem(s + n_pipe - 1, n_pipe), lax.rem(s + 1, n_pipe)
    mirror = n_pipe - 1 - s

    def cols_of(i):
        return pl.ds(pl.multiple_of(i * CHUNK, CHUNK), CHUNK)

    def loads(i):
        cols = cols_of(i)
        return [
            pltpu.make_async_copy(src.at[:, cols], dst.at[:, cols], load_sem.at[k, i])
            for k, (src, dst) in enumerate(((query, q_v), (inner, u_v), (out_grad, g_v)))
        ]

    filter_load = pltpu.make_async_copy(filters, f_v, filter_sem)
    filter_load.start()
    for i in range(2):
        for load in loads(i):
            load.start()

    barrier = pltpu.get_barrier_semaphore()
    for other in (before, after, mirror):
        pl.semaphore_signal(barrier, inc=1, device_id={"pipe": other}, device_id_type=MESH)
    for d in range(1, n_ctx):
        pl.semaphore_signal(barrier, inc=1, device_id={"ctx": lax.rem(c + d, n_ctx)}, device_id_type=MESH)

    ends = []
    for k in range(n_seg):
        ends.append(lengths[0, k] + (ends[-1] if ends else 0))
    pos = c * rows + lax.broadcasted_iota(jnp.int32, (rows + EDGE, LANES), 0)

    def seg_of(at):
        return sum((at >= end).astype(jnp.int32) for end in ends)

    seg = seg_of(pos)
    for j in range(1, taps):
        masks[j - 1] = (seg == seg_of(pos - j)).astype(jnp.float32)

    def back(j, base, mask_at):
        x = u_f[base - j : base - j + EDGE]
        return x if j == 0 else x * masks[j - 1, mask_at : mask_at + EDGE]

    def ahead(j, base, mask_at):
        x = gz_f[base + j : base + j + EDGE]
        return x if j == 0 else x * masks[j - 1, mask_at + j : mask_at + j + EDGE]

    def taps_at(cols):
        return [jnp.broadcast_to(f_v[j, :, cols], (EDGE, LANES)) for j in range(taps)]

    def interior(i):
        def group(l, carry):
            cols = pl.ds(pl.multiple_of(i * CHUNK + l * LANES, LANES), LANES)
            u_f[EDGE : EDGE + rows] = u_v[:, cols].astype(jnp.float32)
            gz_f[:rows] = rounded_product(g_v[:, cols], q_v[:, cols])
            f = taps_at(cols)
            sums = [jnp.zeros((EDGE // 2, LANES), jnp.float32)] * taps
            for at in range(0, rows, EDGE):
                if at > 0:
                    gz = gz_f[at : at + EDGE]
                    z = None
                    for j in range(taps):
                        u = back(j, EDGE + at, at)
                        z = f[j] * u if z is None else z + f[j] * u
                        sums[j] = sums[j] + fold(gz * u)
                    staged[0, at : at + EDGE, cols] = (g_v[at : at + EDGE, cols].astype(jnp.float32) * z).astype(jnp.bfloat16)
                if at < rows - EDGE:
                    z = f[0] * ahead(0, at, at)
                    for j in range(1, taps):
                        z = z + f[j] * ahead(j, at, at)
                    staged[1, at : at + EDGE, cols] = z.astype(jnp.bfloat16)
            for j in range(taps):
                parts[j, :, cols] = sums[j]
            return carry

        lax.fori_loop(0, CHUNK // LANES, group, 0)

    def edges(l, carry):
        cols = pl.ds(pl.multiple_of(l * LANES, LANES), LANES)
        f = taps_at(cols)
        u_f[:EDGE] = u_left[:, cols].astype(jnp.float32)
        u_f[EDGE : 2 * EDGE] = u_v[:EDGE, cols].astype(jnp.float32)
        gz_f[:EDGE] = rounded_product(g_v[rows - EDGE :, cols], q_v[rows - EDGE :, cols])
        gz_f[EDGE : 2 * EDGE] = rounded_product(g_right[:, cols], q_right[:, cols])
        gz = rounded_product(g_v[:EDGE, cols], q_v[:EDGE, cols])
        z = None
        for j in range(taps):
            u = back(j, EDGE, 0)
            z = f[j] * u if z is None else z + f[j] * u
            dh[j : j + 1, cols] = jnp.sum(parts[j, :, cols] + fold(gz * u), axis=0, keepdims=True)
        staged[0, :EDGE, cols] = (g_v[:EDGE, cols].astype(jnp.float32) * z).astype(jnp.bfloat16)
        z = f[0] * ahead(0, 0, rows - EDGE)
        for j in range(1, taps):
            z = z + f[j] * ahead(j, 0, rows - EDGE)
        staged[1, rows - EDGE :, cols] = z.astype(jnp.bfloat16)
        return carry

    def sends(i):
        cols = cols_of(i)
        return [
            pltpu.make_async_remote_copy(
                src_ref=staged.at[k, at, cols], dst_ref=arrived.at[k, 0, at, cols],
                send_sem=out_send.at[k, i], recv_sem=out_recv.at[k, i],
                device_id={"pipe": before}, device_id_type=MESH,
            )
            for k, at in enumerate((pl.ds(EDGE, rows - EDGE), pl.ds(0, rows - EDGE)))
        ]

    def edge_sends():
        return [
            pltpu.make_async_remote_copy(
                src_ref=staged.at[k, at], dst_ref=arrived.at[k, 0, at],
                send_sem=edge_send.at[k], recv_sem=edge_recv.at[k],
                device_id={"pipe": before}, device_id_type=MESH,
            )
            for k, at in enumerate((pl.ds(0, EDGE), pl.ds(rows - EDGE, EDGE)))
        ]

    def halo(k, src, dst, other):
        return pltpu.make_async_remote_copy(
            src_ref=src, dst_ref=dst, send_sem=halo_send.at[k], recv_sem=halo_recv.at[k],
            device_id={"ctx": other}, device_id_type=MESH,
        )

    to_right = [halo(0, inner.at[pl.ds(rows - EDGE, EDGE)], u_left, lax.rem(c + 1, n_ctx))]
    to_left = [
        halo(1, query.at[pl.ds(0, EDGE)], q_right, lax.rem(c + n_ctx - 1, n_ctx)),
        halo(2, out_grad.at[pl.ds(0, EDGE)], g_right, lax.rem(c + n_ctx - 1, n_ctx)),
    ]

    def step(i, carry):
        @pl.when(i + 2 < chunks)
        def _():
            for load in loads(i + 2):
                load.start()

        for load in loads(i):
            load.wait()
        interior(i)

        @pl.when(jnp.logical_not(first))
        def _():
            for send in sends(i):
                send.start()

        return carry

    filter_load.wait()
    for load in loads(2):
        load.start()
    for load in loads(0):
        load.wait()
    interior(0)
    pl.semaphore_wait(barrier, 3 + n_ctx - 1)

    @pl.when(jnp.logical_not(first))
    def _():
        for send in sends(0):
            send.start()

    @pl.when(c < n_ctx - 1)
    def _():
        for send in to_right:
            send.start()

    @pl.when(c > 0)
    def _():
        for send in to_left:
            send.start()

    @pl.when(c == 0)
    def _():
        u_left[...] = jnp.zeros_like(u_left)

    @pl.when(c == n_ctx - 1)
    def _():
        q_right[...] = jnp.zeros_like(q_right)
        g_right[...] = jnp.zeros_like(g_right)

    lax.fori_loop(1, chunks, step, 0)

    @pl.when(c > 0)
    def _():
        for send in to_right:
            send.wait_recv()

    @pl.when(c < n_ctx - 1)
    def _():
        for send in to_left:
            send.wait_recv()

    dh[...] = jnp.zeros_like(dh)
    lax.fori_loop(0, width // LANES, edges, 0)

    @pl.when(jnp.logical_not(first))
    def _():
        for send in edge_sends():
            send.start()

    shares = []
    for d in range(1, n_ctx):
        other = lax.rem(c + d, n_ctx)
        shares.append(
            pltpu.make_async_remote_copy(
                src_ref=dh.at[:, pl.ds(pl.multiple_of(other * own, own), own)], dst_ref=dh_in.at[d - 1],
                send_sem=dh_send.at[d - 1], recv_sem=dh_recv.at[d - 1],
                device_id={"ctx": other}, device_id_type=MESH,
            )
        )
    for share in shares:
        share.start()
    for share in shares:
        share.wait_recv()
    mine = dh[:, pl.ds(pl.multiple_of(c * own, own), own)]
    for d in range(1, n_ctx):
        mine = mine + dh_in[d - 1]
    total[...] = mine
    swap = pltpu.make_async_remote_copy(
        src_ref=total, dst_ref=mirrored, send_sem=mirror_send, recv_sem=mirror_recv,
        device_id={"pipe": mirror}, device_id_type=MESH,
    )
    swap.start()

    @pl.when(last)
    def _():
        arrived[...] = jnp.zeros_like(arrived)

    swap.wait_recv()
    both = total[...] + mirrored[...]
    for j in range(taps):
        summed[j] = both[j : j + 1]
    swap.wait_send()
    for share in shares:
        share.wait_send()

    @pl.when(c < n_ctx - 1)
    def _():
        for send in to_right:
            send.wait_send()

    @pl.when(c > 0)
    def _():
        for send in to_left:
            send.wait_send()

    @pl.when(jnp.logical_not(first))
    def _():
        def drained(i, carry):
            for send in sends(i):
                send.wait_send()
            return carry

        lax.fori_loop(0, chunks, drained, 0)
        for send in edge_sends():
            send.wait_send()

    @pl.when(jnp.logical_not(last))
    def _():
        def landed(i, carry):
            for send in sends(i):
                send.wait_recv()
            return carry

        lax.fori_loop(0, chunks, landed, 0)
        for send in edge_sends():
            send.wait_recv()


def local(n_pipe, n_ctx, query, inner, out_grad, filters, trace_lengths):
    _, rows, width = query.shape
    taps = filters.shape[1]
    own = width // n_ctx
    chunks = width // CHUNK
    anywhere = pl.BlockSpec(memory_space=pl.ANY)
    vmem = pl.BlockSpec(memory_space=pltpu.VMEM)
    f32, bf16, dma = jnp.float32, jnp.bfloat16, pltpu.SemaphoreType.DMA
    arrived, summed = pl.pallas_call(
        functools.partial(kernel, n_pipe, n_ctx, trace_lengths.shape[1]),
        out_shape=(pltpu.VMEM((2, 1, rows, width), bf16), pltpu.VMEM((taps, 1, own), f32)),
        in_specs=[pl.BlockSpec(memory_space=pltpu.SMEM)] + [anywhere] * 4,
        out_specs=(vmem, vmem),
        scratch_shapes=[
            pltpu.VMEM((rows, width), bf16),
            pltpu.VMEM((rows, width), bf16),
            pltpu.VMEM((rows, width), bf16),
            pltpu.VMEM((taps, 1, width), f32),
            pltpu.VMEM((EDGE, width), bf16),
            pltpu.VMEM((EDGE, width), bf16),
            pltpu.VMEM((EDGE, width), bf16),
            pltpu.VMEM((rows + EDGE, LANES), f32),
            pltpu.VMEM((rows + EDGE, LANES), f32),
            pltpu.VMEM((taps - 1, rows + EDGE, LANES), f32),
            pltpu.VMEM((taps, EDGE // 2, width), f32),
            pltpu.VMEM((2, rows, width), bf16),
            pltpu.VMEM((8, width), f32),
            pltpu.VMEM((n_ctx - 1, 8, own), f32),
            pltpu.VMEM((8, own), f32),
            pltpu.VMEM((8, own), f32),
            dma((3, chunks)),
            dma,
            dma((3,)),
            dma((3,)),
            dma((2, chunks)),
            dma((2, chunks)),
            dma((2,)),
            dma((2,)),
            dma((n_ctx - 1,)),
            dma((n_ctx - 1,)),
            dma,
            dma,
        ],
        compiler_params=pltpu.CompilerParams(collective_id=0, has_side_effects=True, vmem_limit_bytes=48 * 1024 * 1024),
        name="grads_passed_on",
    )(trace_lengths, query[0], inner[0], out_grad[0], jnp.swapaxes(filters, 0, 1))
    return arrived, jnp.swapaxes(summed, 0, 1)


def solution(mesh):
    in_specs = (
        P("pipe", "ctx", None),
        P("pipe", "ctx", None),
        P("pipe", "ctx", None),
        P("pipe", None, None),
        P("pipe", None),
    )
    out_specs = (P(None, "pipe", "ctx", None), P("pipe", None, "ctx"))
    run = functools.partial(local, mesh.shape["pipe"], mesh.shape["ctx"])
    return jax.shard_map(run, mesh=mesh, in_specs=in_specs, out_specs=out_specs, check_vma=False)
```

```python
import functools

import jax
import jax.numpy as jnp
from jax import lax
from jax.experimental import pallas as pl
from jax.experimental.pallas import tpu as pltpu
from jax.sharding import PartitionSpec as P

MESH = pl.DeviceIdType.MESH
EDGE = 16
LANES = 128
CHUNK = 512


def fold(x):
    return x[: EDGE // 2] + x[EDGE // 2 :]


def rounded_product(a, b):
    return (a.astype(jnp.float32) * b.astype(jnp.float32)).astype(jnp.bfloat16).astype(jnp.float32)


def kernel(
    n_pipe, n_ctx, n_seg,
    trace_lengths, query, inner, out_grad, filters, arrived, summed,
    lengths, q_v, u_v, g_v, f_v, u_left, q_right, g_right, u_f, gz_f, masks, parts, staged, dh, dh_in, total, mirrored,
    length_sem, load_sem, filter_sem, halo_send, halo_recv, out_send, out_recv, edge_send, edge_recv, dh_send, dh_recv, mirror_send, mirror_recv,
):
    taps, _, width = filters.shape
    rows = query.shape[0]
    own = width // n_ctx
    chunks = width // CHUNK
    early = chunks * 10 // 16
    s = lax.axis_index("pipe")
    c = lax.axis_index("ctx")
    first, last = s == 0, s == n_pipe - 1
    before, after = lax.rem(s + n_pipe - 1, n_pipe), lax.rem(s + 1, n_pipe)
    mirror = n_pipe - 1 - s

    def cols_of(i):
        return pl.ds(pl.multiple_of(i * CHUNK, CHUNK), CHUNK)

    def loads(i):
        cols = cols_of(i)
        return [
            pltpu.make_async_copy(src.at[:, cols], dst.at[:, cols], load_sem.at[k, i])
            for k, (src, dst) in enumerate(((query, q_v), (inner, u_v), (out_grad, g_v)))
        ]

    length_load = pltpu.make_async_copy(trace_lengths, lengths, length_sem)
    length_load.start()
    filter_load = pltpu.make_async_copy(filters, f_v, filter_sem)
    filter_load.start()
    for i in range(2):
        for load in loads(i):
            load.start()

    barrier = pltpu.get_barrier_semaphore()
    for other in (before, after, mirror):
        pl.semaphore_signal(barrier, inc=1, device_id={"pipe": other}, device_id_type=MESH)
    for d in range(1, n_ctx):
        pl.semaphore_signal(barrier, inc=1, device_id={"ctx": lax.rem(c + d, n_ctx)}, device_id_type=MESH)

    length_load.wait()
    ends = []
    for k in range(n_seg):
        ends.append(lengths[0, k] + (ends[-1] if ends else 0))
    pos = c * rows + lax.broadcasted_iota(jnp.int32, (rows + EDGE, LANES), 0)

    def seg_of(at):
        return sum((at >= end).astype(jnp.int32) for end in ends)

    seg = seg_of(pos)
    for j in range(1, taps):
        masks[j - 1] = (seg == seg_of(pos - j)).astype(jnp.float32)

    def back(j, base, mask_at):
        x = u_f[base - j : base - j + EDGE]
        return x if j == 0 else x * masks[j - 1, mask_at : mask_at + EDGE]

    def ahead(j, base, mask_at):
        x = gz_f[base + j : base + j + EDGE]
        return x if j == 0 else x * masks[j - 1, mask_at + j : mask_at + j + EDGE]

    def taps_at(cols):
        return [jnp.broadcast_to(f_v[j, :, cols], (EDGE, LANES)) for j in range(taps)]

    def interior(i):
        def group(l, carry):
            cols = pl.ds(pl.multiple_of(i * CHUNK + l * LANES, LANES), LANES)
            u_f[EDGE : EDGE + rows] = u_v[:, cols].astype(jnp.float32)
            gz_f[:rows] = rounded_product(g_v[:, cols], q_v[:, cols])
            f = taps_at(cols)
            sums = [jnp.zeros((EDGE // 2, LANES), jnp.float32)] * taps
            for at in range(0, rows, EDGE):
                if at > 0:
                    gz = gz_f[at : at + EDGE]
                    z = None
                    for j in range(taps):
                        u = back(j, EDGE + at, at)
                        z = f[j] * u if z is None else z + f[j] * u
                        sums[j] = sums[j] + fold(gz * u)
                    staged[0, at : at + EDGE, cols] = (g_v[at : at + EDGE, cols].astype(jnp.float32) * z).astype(jnp.bfloat16)
                if at < rows - EDGE:
                    z = f[0] * ahead(0, at, at)
                    for j in range(1, taps):
                        z = z + f[j] * ahead(j, at, at)
                    staged[1, at : at + EDGE, cols] = z.astype(jnp.bfloat16)
            for j in range(taps):
                parts[j, :, cols] = sums[j]
            return carry

        lax.fori_loop(0, CHUNK // LANES, group, 0)

    def edges(l, carry):
        cols = pl.ds(pl.multiple_of(l * LANES, LANES), LANES)
        f = taps_at(cols)
        u_f[:EDGE] = u_left[:, cols].astype(jnp.float32)
        u_f[EDGE : 2 * EDGE] = u_v[:EDGE, cols].astype(jnp.float32)
        gz_f[:EDGE] = rounded_product(g_v[rows - EDGE :, cols], q_v[rows - EDGE :, cols])
        gz_f[EDGE : 2 * EDGE] = rounded_product(g_right[:, cols], q_right[:, cols])
        gz = rounded_product(g_v[:EDGE, cols], q_v[:EDGE, cols])
        z = None
        for j in range(taps):
            u = back(j, EDGE, 0)
            z = f[j] * u if z is None else z + f[j] * u
            dh[j : j + 1, cols] = jnp.sum(parts[j, :, cols] + fold(gz * u), axis=0, keepdims=True)
        staged[0, :EDGE, cols] = (g_v[:EDGE, cols].astype(jnp.float32) * z).astype(jnp.bfloat16)
        z = f[0] * ahead(0, 0, rows - EDGE)
        for j in range(1, taps):
            z = z + f[j] * ahead(j, 0, rows - EDGE)
        staged[1, rows - EDGE :, cols] = z.astype(jnp.bfloat16)
        return carry

    def sends(i):
        cols = cols_of(i)
        return [
            pltpu.make_async_remote_copy(
                src_ref=staged.at[k, at, cols], dst_ref=arrived.at[k, 0, at, cols],
                send_sem=out_send.at[k, i], recv_sem=out_recv.at[k, i],
                device_id={"pipe": before}, device_id_type=MESH,
            )
            for k, at in enumerate((pl.ds(EDGE, rows - EDGE), pl.ds(0, rows - EDGE)))
        ]

    def edge_sends():
        return [
            pltpu.make_async_remote_copy(
                src_ref=staged.at[k, at], dst_ref=arrived.at[k, 0, at],
                send_sem=edge_send.at[k], recv_sem=edge_recv.at[k],
                device_id={"pipe": before}, device_id_type=MESH,
            )
            for k, at in enumerate((pl.ds(0, EDGE), pl.ds(rows - EDGE, EDGE)))
        ]

    def halo(k, src, dst, other):
        return pltpu.make_async_remote_copy(
            src_ref=src, dst_ref=dst, send_sem=halo_send.at[k], recv_sem=halo_recv.at[k],
            device_id={"ctx": other}, device_id_type=MESH,
        )

    to_right = [halo(0, inner.at[pl.ds(rows - EDGE, EDGE)], u_left, lax.rem(c + 1, n_ctx))]
    to_left = [
        halo(1, query.at[pl.ds(0, EDGE)], q_right, lax.rem(c + n_ctx - 1, n_ctx)),
        halo(2, out_grad.at[pl.ds(0, EDGE)], g_right, lax.rem(c + n_ctx - 1, n_ctx)),
    ]

    def step(i, carry):
        @pl.when(i + 2 < chunks)
        def _():
            for load in loads(i + 2):
                load.start()

        for load in loads(i):
            load.wait()
        interior(i)

        @pl.when(jnp.logical_and(jnp.logical_not(first), i < early))
        def _():
            for send in sends(i):
                send.start()

        return carry

    filter_load.wait()
    for load in loads(2):
        load.start()
    for load in loads(0):
        load.wait()
    interior(0)
    pl.semaphore_wait(barrier, 3 + n_ctx - 1)

    @pl.when(jnp.logical_not(first))
    def _():
        for send in sends(0):
            send.start()

    @pl.when(c < n_ctx - 1)
    def _():
        for send in to_right:
            send.start()

    @pl.when(c > 0)
    def _():
        for send in to_left:
            send.start()

    @pl.when(c == 0)
    def _():
        u_left[...] = jnp.zeros_like(u_left)

    @pl.when(c == n_ctx - 1)
    def _():
        q_right[...] = jnp.zeros_like(q_right)
        g_right[...] = jnp.zeros_like(g_right)

    lax.fori_loop(1, chunks, step, 0)

    @pl.when(c > 0)
    def _():
        for send in to_right:
            send.wait_recv()

    @pl.when(c < n_ctx - 1)
    def _():
        for send in to_left:
            send.wait_recv()

    dh[...] = jnp.zeros_like(dh)
    lax.fori_loop(0, width // LANES, edges, 0)

    shares = []
    for d in range(1, n_ctx):
        other = lax.rem(c + d, n_ctx)
        shares.append(
            pltpu.make_async_remote_copy(
                src_ref=dh.at[:, pl.ds(pl.multiple_of(other * own, own), own)], dst_ref=dh_in.at[d - 1],
                send_sem=dh_send.at[d - 1], recv_sem=dh_recv.at[d - 1],
                device_id={"ctx": other}, device_id_type=MESH,
            )
        )
    for share in shares:
        share.start()
    for share in shares:
        share.wait_recv()
    mine = dh[:, pl.ds(pl.multiple_of(c * own, own), own)]
    for d in range(1, n_ctx):
        mine = mine + dh_in[d - 1]
    half = own // 2
    total[...] = jnp.concatenate([mine[:, :half], mine[:, half:]], axis=0).astype(jnp.bfloat16)
    swap = pltpu.make_async_remote_copy(
        src_ref=total, dst_ref=mirrored, send_sem=mirror_send, recv_sem=mirror_recv,
        device_id={"pipe": mirror}, device_id_type=MESH,
    )
    swap.start()

    @pl.when(jnp.logical_not(first))
    def _():
        def late(i, carry):
            for send in sends(i):
                send.start()
            return carry

        lax.fori_loop(early, chunks, late, 0)
        for send in edge_sends():
            send.start()

    @pl.when(last)
    def _():
        arrived[...] = jnp.zeros_like(arrived)

    swap.wait_recv()
    theirs = mirrored[...].astype(jnp.float32)
    for j in range(taps):
        summed[j, :, :half] = mine[j : j + 1, :half] + theirs[j : j + 1]
        summed[j, :, half:] = mine[j : j + 1, half:] + theirs[8 + j : 9 + j]
    swap.wait_send()
    for share in shares:
        share.wait_send()

    @pl.when(c < n_ctx - 1)
    def _():
        for send in to_right:
            send.wait_send()

    @pl.when(c > 0)
    def _():
        for send in to_left:
            send.wait_send()

    @pl.when(jnp.logical_not(first))
    def _():
        def drained(i, carry):
            for send in sends(i):
                send.wait_send()
            return carry

        lax.fori_loop(0, chunks, drained, 0)
        for send in edge_sends():
            send.wait_send()

    @pl.when(jnp.logical_not(last))
    def _():
        def landed(i, carry):
            for send in sends(i):
                send.wait_recv()
            return carry

        lax.fori_loop(0, chunks, landed, 0)
        for send in edge_sends():
            send.wait_recv()


def local(n_pipe, n_ctx, query, inner, out_grad, filters, trace_lengths):
    _, rows, width = query.shape
    taps = filters.shape[1]
    own = width // n_ctx
    chunks = width // CHUNK
    vmem = pl.BlockSpec(memory_space=pltpu.VMEM)
    operands = (trace_lengths, query[0], inner[0], out_grad[0], jnp.swapaxes(filters, 0, 1))
    f32, bf16, dma = jnp.float32, jnp.bfloat16, pltpu.SemaphoreType.DMA
    arrived, summed = pl.pallas_call(
        functools.partial(kernel, n_pipe, n_ctx, trace_lengths.shape[1]),
        out_shape=(pltpu.VMEM((2, 1, rows, width), bf16), pltpu.VMEM((taps, 1, own), f32)),
        in_specs=[pl.BlockSpec(memory_space=pltpu.HBM)] * 5,
        out_specs=(vmem, vmem),
        scratch_shapes=[
            pltpu.SMEM(trace_lengths.shape, jnp.int32),
            pltpu.VMEM((rows, width), bf16),
            pltpu.VMEM((rows, width), bf16),
            pltpu.VMEM((rows, width), bf16),
            pltpu.VMEM((taps, 1, width), f32),
            pltpu.VMEM((EDGE, width), bf16),
            pltpu.VMEM((EDGE, width), bf16),
            pltpu.VMEM((EDGE, width), bf16),
            pltpu.VMEM((rows + EDGE, LANES), f32),
            pltpu.VMEM((rows + EDGE, LANES), f32),
            pltpu.VMEM((taps - 1, rows + EDGE, LANES), f32),
            pltpu.VMEM((taps, EDGE // 2, width), f32),
            pltpu.VMEM((2, rows, width), bf16),
            pltpu.VMEM((8, width), f32),
            pltpu.VMEM((n_ctx - 1, 8, own), f32),
            pltpu.VMEM((16, own // 2), bf16),
            pltpu.VMEM((16, own // 2), bf16),
            dma,
            dma((3, chunks)),
            dma,
            dma((3,)),
            dma((3,)),
            dma((2, chunks)),
            dma((2, chunks)),
            dma((2,)),
            dma((2,)),
            dma((n_ctx - 1,)),
            dma((n_ctx - 1,)),
            dma,
            dma,
        ],
        compiler_params=pltpu.CompilerParams(collective_id=0, has_side_effects=True, vmem_limit_bytes=48 * 1024 * 1024),
        name="grads_passed_on",
    )(*(pltpu.with_memory_space_constraint(x, pltpu.HBM) for x in operands))
    return arrived, jnp.swapaxes(summed, 0, 1)


def solution(mesh):
    in_specs = (
        P("pipe", "ctx", None),
        P("pipe", "ctx", None),
        P("pipe", "ctx", None),
        P("pipe", None, None),
        P("pipe", None),
    )
    out_specs = (P(None, "pipe", "ctx", None), P("pipe", None, "ctx"))
    run = functools.partial(local, mesh.shape["pipe"], mesh.shape["ctx"])
    return jax.shard_map(run, mesh=mesh, in_specs=in_specs, out_specs=out_specs, check_vma=False)
```

```python
import functools

import jax
import jax.numpy as jnp
from jax import lax
from jax.experimental import pallas as pl
from jax.experimental.pallas import tpu as pltpu
from jax.sharding import PartitionSpec as P

MESH = pl.DeviceIdType.MESH
EDGE = 16
LANES = 128
FIRST_GROUPS = (256, 256, 512, 1024)
GROUP = 2048


def groups_of(width):
    sizes = list(FIRST_GROUPS)
    while sum(sizes) < width:
        sizes.append(min(GROUP, width - sum(sizes)))
    return [(sum(sizes[:i]), size) for i, size in enumerate(sizes)]


def fold(x):
    return x[: EDGE // 2] + x[EDGE // 2 :]


def rounded_product(a, b):
    return (a.astype(jnp.float32) * b.astype(jnp.float32)).astype(jnp.bfloat16).astype(jnp.float32)


def kernel(
    n_pipe, n_ctx, n_seg,
    trace_lengths, query, inner, out_grad, filters, arrived, summed,
    lengths, q_v, u_v, g_v, f_v, u_left, q_right, g_right, u_f, gz_f, masks, parts, staged, dh, dh_in, total, mirrored,
    length_sem, load_sem, filter_sem, halo_send, halo_recv, out_send, out_recv, edge_send, edge_recv, dh_send, dh_recv, mirror_send, mirror_recv,
):
    taps, _, width = filters.shape
    rows = query.shape[0]
    own = width // n_ctx
    groups = groups_of(width)
    early = sum(start < width // 2 for start, _ in groups)
    s = lax.axis_index("pipe")
    c = lax.axis_index("ctx")
    first, last = s == 0, s == n_pipe - 1
    before, after = lax.rem(s + n_pipe - 1, n_pipe), lax.rem(s + 1, n_pipe)
    mirror = n_pipe - 1 - s

    def cols_of(i):
        return pl.ds(*groups[i])

    def loads(i):
        cols = cols_of(i)
        return [
            pltpu.make_async_copy(src.at[:, cols], dst.at[:, cols], load_sem.at[k, i])
            for k, (src, dst) in enumerate(((query, q_v), (inner, u_v), (out_grad, g_v)))
        ]

    length_load = pltpu.make_async_copy(trace_lengths, lengths, length_sem)
    length_load.start()
    filter_load = pltpu.make_async_copy(filters, f_v, filter_sem)
    filter_load.start()
    for i in range(3):
        for load in loads(i):
            load.start()

    barrier = pltpu.get_barrier_semaphore()
    for other in (before, after, mirror):
        pl.semaphore_signal(barrier, inc=1, device_id={"pipe": other}, device_id_type=MESH)
    for d in range(1, n_ctx):
        pl.semaphore_signal(barrier, inc=1, device_id={"ctx": lax.rem(c + d, n_ctx)}, device_id_type=MESH)

    length_load.wait()
    ends = []
    for k in range(n_seg):
        ends.append(lengths[0, k] + (ends[-1] if ends else 0))
    pos = c * rows + lax.broadcasted_iota(jnp.int32, (rows + EDGE, LANES), 0)

    def seg_of(at):
        return sum((at >= end).astype(jnp.int32) for end in ends)

    seg = seg_of(pos)
    for j in range(1, taps):
        masks[j - 1] = (seg == seg_of(pos - j)).astype(jnp.float32)

    def back(j, base, mask_at):
        x = u_f[base - j : base - j + EDGE]
        return x if j == 0 else x * masks[j - 1, mask_at : mask_at + EDGE]

    def ahead(j, base, mask_at):
        x = gz_f[base + j : base + j + EDGE]
        return x if j == 0 else x * masks[j - 1, mask_at + j : mask_at + j + EDGE]

    def taps_at(cols):
        return [jnp.broadcast_to(f_v[j, :, cols], (EDGE, LANES)) for j in range(taps)]

    def interior(i):
        def group(l, carry):
            cols = pl.ds(pl.multiple_of(groups[i][0] + l * LANES, LANES), LANES)
            u_f[EDGE : EDGE + rows] = u_v[:, cols].astype(jnp.float32)
            gz_f[:rows] = rounded_product(g_v[:, cols], q_v[:, cols])
            f = taps_at(cols)
            sums = [jnp.zeros((EDGE // 2, LANES), jnp.float32)] * taps
            for at in range(0, rows, EDGE):
                if at > 0:
                    gz = gz_f[at : at + EDGE]
                    z = None
                    for j in range(taps):
                        u = back(j, EDGE + at, at)
                        z = f[j] * u if z is None else z + f[j] * u
                        sums[j] = sums[j] + fold(gz * u)
                    staged[0, at : at + EDGE, cols] = (g_v[at : at + EDGE, cols].astype(jnp.float32) * z).astype(jnp.bfloat16)
                if at < rows - EDGE:
                    z = f[0] * ahead(0, at, at)
                    for j in range(1, taps):
                        z = z + f[j] * ahead(j, at, at)
                    staged[1, at : at + EDGE, cols] = z.astype(jnp.bfloat16)
            for j in range(taps):
                parts[j, :, cols] = sums[j]
            return carry

        lax.fori_loop(0, groups[i][1] // LANES, group, 0)

    def edges(l, carry):
        cols = pl.ds(pl.multiple_of(l * LANES, LANES), LANES)
        f = taps_at(cols)
        u_f[:EDGE] = u_left[:, cols].astype(jnp.float32)
        u_f[EDGE : 2 * EDGE] = u_v[:EDGE, cols].astype(jnp.float32)
        gz_f[:EDGE] = rounded_product(g_v[rows - EDGE :, cols], q_v[rows - EDGE :, cols])
        gz_f[EDGE : 2 * EDGE] = rounded_product(g_right[:, cols], q_right[:, cols])
        gz = rounded_product(g_v[:EDGE, cols], q_v[:EDGE, cols])
        z = None
        for j in range(taps):
            u = back(j, EDGE, 0)
            z = f[j] * u if z is None else z + f[j] * u
            dh[j : j + 1, cols] = jnp.sum(parts[j, :, cols] + fold(gz * u), axis=0, keepdims=True)
        staged[0, :EDGE, cols] = (g_v[:EDGE, cols].astype(jnp.float32) * z).astype(jnp.bfloat16)
        z = f[0] * ahead(0, 0, rows - EDGE)
        for j in range(1, taps):
            z = z + f[j] * ahead(j, 0, rows - EDGE)
        staged[1, rows - EDGE :, cols] = z.astype(jnp.bfloat16)
        return carry

    def sends(i):
        cols = cols_of(i)
        return [
            pltpu.make_async_remote_copy(
                src_ref=staged.at[k, at, cols], dst_ref=arrived.at[k, 0, at, cols],
                send_sem=out_send.at[k, i], recv_sem=out_recv.at[k, i],
                device_id={"pipe": before}, device_id_type=MESH,
            )
            for k, at in enumerate((pl.ds(EDGE, rows - EDGE), pl.ds(0, rows - EDGE)))
        ]

    def edge_sends():
        return [
            pltpu.make_async_remote_copy(
                src_ref=staged.at[k, at], dst_ref=arrived.at[k, 0, at],
                send_sem=edge_send.at[k], recv_sem=edge_recv.at[k],
                device_id={"pipe": before}, device_id_type=MESH,
            )
            for k, at in enumerate((pl.ds(0, EDGE), pl.ds(rows - EDGE, EDGE)))
        ]

    def halo(k, src, dst, other):
        return pltpu.make_async_remote_copy(
            src_ref=src, dst_ref=dst, send_sem=halo_send.at[k], recv_sem=halo_recv.at[k],
            device_id={"ctx": other}, device_id_type=MESH,
        )

    to_right = [halo(0, inner.at[pl.ds(rows - EDGE, EDGE)], u_left, lax.rem(c + 1, n_ctx))]
    to_left = [
        halo(1, query.at[pl.ds(0, EDGE)], q_right, lax.rem(c + n_ctx - 1, n_ctx)),
        halo(2, out_grad.at[pl.ds(0, EDGE)], g_right, lax.rem(c + n_ctx - 1, n_ctx)),
    ]

    filter_load.wait()
    for load in loads(0):
        load.wait()
    interior(0)
    pl.semaphore_wait(barrier, 3 + n_ctx - 1)

    @pl.when(jnp.logical_not(first))
    def _():
        for send in sends(0):
            send.start()

    for i in range(3, len(groups)):
        for load in loads(i):
            load.start()

    @pl.when(c < n_ctx - 1)
    def _():
        for send in to_right:
            send.start()

    @pl.when(c > 0)
    def _():
        for send in to_left:
            send.start()

    @pl.when(c == 0)
    def _():
        u_left[...] = jnp.zeros_like(u_left)

    @pl.when(c == n_ctx - 1)
    def _():
        q_right[...] = jnp.zeros_like(q_right)
        g_right[...] = jnp.zeros_like(g_right)

    for i in range(1, len(groups)):
        for load in loads(i):
            load.wait()
        interior(i)
        if i < early:

            @pl.when(jnp.logical_not(first))
            def _():
                for send in sends(i):
                    send.start()

    @pl.when(c > 0)
    def _():
        for send in to_right:
            send.wait_recv()

    @pl.when(c < n_ctx - 1)
    def _():
        for send in to_left:
            send.wait_recv()

    dh[...] = jnp.zeros_like(dh)
    lax.fori_loop(0, width // LANES, edges, 0)

    @pl.when(jnp.logical_not(first))
    def _():
        for send in edge_sends():
            send.start()

    shares = []
    for d in range(1, n_ctx):
        other = lax.rem(c + d, n_ctx)
        shares.append(
            pltpu.make_async_remote_copy(
                src_ref=dh.at[:, pl.ds(pl.multiple_of(other * own, own), own)], dst_ref=dh_in.at[d - 1],
                send_sem=dh_send.at[d - 1], recv_sem=dh_recv.at[d - 1],
                device_id={"ctx": other}, device_id_type=MESH,
            )
        )
    for share in shares:
        share.start()
    for share in shares:
        share.wait_recv()
    mine = dh[:, pl.ds(pl.multiple_of(c * own, own), own)]
    for d in range(1, n_ctx):
        mine = mine + dh_in[d - 1]
    half = own // 2
    total[...] = jnp.concatenate([mine[:, :half], mine[:, half:]], axis=0).astype(jnp.bfloat16)
    swap = pltpu.make_async_remote_copy(
        src_ref=total, dst_ref=mirrored, send_sem=mirror_send, recv_sem=mirror_recv,
        device_id={"pipe": mirror}, device_id_type=MESH,
    )
    swap.start()

    @pl.when(jnp.logical_not(first))
    def _():
        for i in range(early, len(groups)):
            for send in sends(i):
                send.start()

    @pl.when(last)
    def _():
        arrived[...] = jnp.zeros_like(arrived)

    swap.wait_recv()
    theirs = mirrored[...].astype(jnp.float32)
    for j in range(taps):
        summed[j, :, :half] = mine[j : j + 1, :half] + theirs[j : j + 1]
        summed[j, :, half:] = mine[j : j + 1, half:] + theirs[8 + j : 9 + j]
    swap.wait_send()
    for share in shares:
        share.wait_send()

    @pl.when(c < n_ctx - 1)
    def _():
        for send in to_right:
            send.wait_send()

    @pl.when(c > 0)
    def _():
        for send in to_left:
            send.wait_send()

    @pl.when(jnp.logical_not(first))
    def _():
        for i in range(len(groups)):
            for send in sends(i):
                send.wait_send()
        for send in edge_sends():
            send.wait_send()

    @pl.when(jnp.logical_not(last))
    def _():
        for i in range(len(groups)):
            for send in sends(i):
                send.wait_recv()
        for send in edge_sends():
            send.wait_recv()


def local(n_pipe, n_ctx, query, inner, out_grad, filters, trace_lengths):
    _, rows, width = query.shape
    taps = filters.shape[1]
    own = width // n_ctx
    groups = len(groups_of(width))
    vmem = pl.BlockSpec(memory_space=pltpu.VMEM)
    operands = (trace_lengths, query[0], inner[0], out_grad[0], jnp.swapaxes(filters, 0, 1))
    f32, bf16, dma = jnp.float32, jnp.bfloat16, pltpu.SemaphoreType.DMA
    arrived, summed = pl.pallas_call(
        functools.partial(kernel, n_pipe, n_ctx, trace_lengths.shape[1]),
        out_shape=(pltpu.VMEM((2, 1, rows, width), bf16), pltpu.VMEM((taps, 1, own), f32)),
        in_specs=[pl.BlockSpec(memory_space=pltpu.HBM)] * 5,
        out_specs=(vmem, vmem),
        scratch_shapes=[
            pltpu.SMEM(trace_lengths.shape, jnp.int32),
            pltpu.VMEM((rows, width), bf16),
            pltpu.VMEM((rows, width), bf16),
            pltpu.VMEM((rows, width), bf16),
            pltpu.VMEM((taps, 1, width), f32),
            pltpu.VMEM((EDGE, width), bf16),
            pltpu.VMEM((EDGE, width), bf16),
            pltpu.VMEM((EDGE, width), bf16),
            pltpu.VMEM((rows + EDGE, LANES), f32),
            pltpu.VMEM((rows + EDGE, LANES), f32),
            pltpu.VMEM((taps - 1, rows + EDGE, LANES), f32),
            pltpu.VMEM((taps, EDGE // 2, width), f32),
            pltpu.VMEM((2, rows, width), bf16),
            pltpu.VMEM((8, width), f32),
            pltpu.VMEM((n_ctx - 1, 8, own), f32),
            pltpu.VMEM((16, own // 2), bf16),
            pltpu.VMEM((16, own // 2), bf16),
            dma,
            dma((3, groups)),
            dma,
            dma((3,)),
            dma((3,)),
            dma((2, groups)),
            dma((2, groups)),
            dma((2,)),
            dma((2,)),
            dma((n_ctx - 1,)),
            dma((n_ctx - 1,)),
            dma,
            dma,
        ],
        compiler_params=pltpu.CompilerParams(collective_id=0, has_side_effects=True, vmem_limit_bytes=48 * 1024 * 1024),
        name="grads_passed_on",
    )(*(pltpu.with_memory_space_constraint(x, pltpu.HBM) for x in operands))
    return arrived, jnp.swapaxes(summed, 0, 1)


def solution(mesh):
    in_specs = (
        P("pipe", "ctx", None),
        P("pipe", "ctx", None),
        P("pipe", "ctx", None),
        P("pipe", None, None),
        P("pipe", None),
    )
    out_specs = (P(None, "pipe", "ctx", None), P("pipe", None, "ctx"))
    run = functools.partial(local, mesh.shape["pipe"], mesh.shape["ctx"])
    return jax.shard_map(run, mesh=mesh, in_specs=in_specs, out_specs=out_specs, check_vma=False)
```

```python
import functools

import jax
import jax.numpy as jnp
from jax import lax
from jax.experimental import pallas as pl
from jax.experimental.pallas import tpu as pltpu
from jax.sharding import PartitionSpec as P

MESH = pl.DeviceIdType.MESH
EDGE = 16
LANES = 128
PARTS = 4
FIRST_GROUPS = (256, 256, 512, 1024)
GROUP = 2048


def groups_of(width):
    sizes = list(FIRST_GROUPS)
    while sum(sizes) < width:
        sizes.append(min(GROUP, width - sum(sizes)))
    return [(sum(sizes[:i]), size) for i, size in enumerate(sizes)]


def fold(x):
    return x[: EDGE // 2] + x[EDGE // 2 :]


def rounded_product(a, b):
    return (a.astype(jnp.float32) * b.astype(jnp.float32)).astype(jnp.bfloat16).astype(jnp.float32)


def kernel(
    n_pipe, n_ctx, n_seg,
    trace_lengths, query, inner, out_grad, filters, arrived, summed,
    lengths, q_v, u_v, g_v, f_v, u_left, q_right, g_right, u_f, gz_f, masks, parts, staged, dh, dh_in, total, mirrored,
    length_sem, load_sem, filter_sem, halo_send, halo_recv, out_send, out_recv, edge_send, edge_recv, dh_send, dh_recv, mirror_send, mirror_recv,
):
    taps, _, width = filters.shape
    rows = query.shape[0]
    own = width // n_ctx
    groups = groups_of(width)
    early = sum(start < width // 2 for start, _ in groups)
    s = lax.axis_index("pipe")
    c = lax.axis_index("ctx")
    first, last = s == 0, s == n_pipe - 1
    before, after = lax.rem(s + n_pipe - 1, n_pipe), lax.rem(s + 1, n_pipe)
    mirror = n_pipe - 1 - s

    def cols_of(i):
        return pl.ds(*groups[i])

    def loads(i):
        cols = cols_of(i)
        return [
            pltpu.make_async_copy(src.at[:, cols], dst.at[:, cols], load_sem.at[k, i])
            for k, (src, dst) in enumerate(((query, q_v), (inner, u_v), (out_grad, g_v)))
        ]

    length_load = pltpu.make_async_copy(trace_lengths, lengths, length_sem)
    length_load.start()
    filter_load = pltpu.make_async_copy(filters, f_v, filter_sem)
    filter_load.start()
    for i in range(3):
        for load in loads(i):
            load.start()

    barrier = pltpu.get_barrier_semaphore()
    for other in (before, after, mirror):
        pl.semaphore_signal(barrier, inc=1, device_id={"pipe": other}, device_id_type=MESH)
    for d in range(1, n_ctx):
        pl.semaphore_signal(barrier, inc=1, device_id={"ctx": lax.rem(c + d, n_ctx)}, device_id_type=MESH)

    length_load.wait()
    ends = []
    for k in range(n_seg):
        ends.append(lengths[0, k] + (ends[-1] if ends else 0))
    pos = c * rows + lax.broadcasted_iota(jnp.int32, (rows + EDGE, LANES), 0)

    def seg_of(at):
        return sum((at >= end).astype(jnp.int32) for end in ends)

    seg = seg_of(pos)
    for j in range(1, taps):
        masks[j - 1] = (seg == seg_of(pos - j)).astype(jnp.float32)

    def back(j, base, mask_at):
        x = u_f[base - j : base - j + EDGE]
        return x if j == 0 else x * masks[j - 1, mask_at : mask_at + EDGE]

    def ahead(j, base, mask_at):
        x = gz_f[base + j : base + j + EDGE]
        return x if j == 0 else x * masks[j - 1, mask_at + j : mask_at + j + EDGE]

    def taps_at(cols):
        return [jnp.broadcast_to(f_v[j, :, cols], (EDGE, LANES)) for j in range(taps)]

    def interior(i):
        def group(l, carry):
            cols = pl.ds(pl.multiple_of(groups[i][0] + l * LANES, LANES), LANES)
            u_f[EDGE : EDGE + rows] = u_v[:, cols].astype(jnp.float32)
            gz_f[:rows] = rounded_product(g_v[:, cols], q_v[:, cols])
            f = taps_at(cols)
            sums = [jnp.zeros((EDGE // 2, LANES), jnp.float32)] * taps
            for at in range(0, rows, EDGE):
                if at > 0:
                    gz = gz_f[at : at + EDGE]
                    z = None
                    for j in range(taps):
                        u = back(j, EDGE + at, at)
                        z = f[j] * u if z is None else z + f[j] * u
                        sums[j] = sums[j] + fold(gz * u)
                    staged[0, at : at + EDGE, cols] = (g_v[at : at + EDGE, cols].astype(jnp.float32) * z).astype(jnp.bfloat16)
                if at < rows - EDGE:
                    z = f[0] * ahead(0, at, at)
                    for j in range(1, taps):
                        z = z + f[j] * ahead(j, at, at)
                    staged[1, at : at + EDGE, cols] = z.astype(jnp.bfloat16)
            for j in range(taps):
                parts[j, :, cols] = sums[j]
            return carry

        lax.fori_loop(0, groups[i][1] // LANES, group, 0)

    def edges(l, carry):
        cols = pl.ds(pl.multiple_of(l * LANES, LANES), LANES)
        f = taps_at(cols)
        u_f[:EDGE] = u_left[:, cols].astype(jnp.float32)
        u_f[EDGE : 2 * EDGE] = u_v[:EDGE, cols].astype(jnp.float32)
        gz_f[:EDGE] = rounded_product(g_v[rows - EDGE :, cols], q_v[rows - EDGE :, cols])
        gz_f[EDGE : 2 * EDGE] = rounded_product(g_right[:, cols], q_right[:, cols])
        gz = rounded_product(g_v[:EDGE, cols], q_v[:EDGE, cols])
        z = None
        for j in range(taps):
            u = back(j, EDGE, 0)
            z = f[j] * u if z is None else z + f[j] * u
            dh[j : j + 1, cols] = jnp.sum(parts[j, :, cols] + fold(gz * u), axis=0, keepdims=True)
        staged[0, :EDGE, cols] = (g_v[:EDGE, cols].astype(jnp.float32) * z).astype(jnp.bfloat16)
        z = f[0] * ahead(0, 0, rows - EDGE)
        for j in range(1, taps):
            z = z + f[j] * ahead(j, 0, rows - EDGE)
        staged[1, rows - EDGE :, cols] = z.astype(jnp.bfloat16)
        return carry

    def sends(i):
        cols = cols_of(i)
        return [
            pltpu.make_async_remote_copy(
                src_ref=staged.at[k, at, cols], dst_ref=arrived.at[k, 0, at, cols],
                send_sem=out_send.at[k, i], recv_sem=out_recv.at[k, i],
                device_id={"pipe": before}, device_id_type=MESH,
            )
            for k, at in enumerate((pl.ds(EDGE, rows - EDGE), pl.ds(0, rows - EDGE)))
        ]

    def edge_sends():
        return [
            pltpu.make_async_remote_copy(
                src_ref=staged.at[k, at], dst_ref=arrived.at[k, 0, at],
                send_sem=edge_send.at[k], recv_sem=edge_recv.at[k],
                device_id={"pipe": before}, device_id_type=MESH,
            )
            for k, at in enumerate((pl.ds(0, EDGE), pl.ds(rows - EDGE, EDGE)))
        ]

    def halo(k, src, dst, other):
        return pltpu.make_async_remote_copy(
            src_ref=src, dst_ref=dst, send_sem=halo_send.at[k], recv_sem=halo_recv.at[k],
            device_id={"ctx": other}, device_id_type=MESH,
        )

    to_right = [halo(0, inner.at[pl.ds(rows - EDGE, EDGE)], u_left, lax.rem(c + 1, n_ctx))]
    to_left = [
        halo(1, query.at[pl.ds(0, EDGE)], q_right, lax.rem(c + n_ctx - 1, n_ctx)),
        halo(2, out_grad.at[pl.ds(0, EDGE)], g_right, lax.rem(c + n_ctx - 1, n_ctx)),
    ]

    filter_load.wait()
    for load in loads(0):
        load.wait()
    interior(0)
    pl.semaphore_wait(barrier, 3 + n_ctx - 1)

    @pl.when(jnp.logical_not(first))
    def _():
        for send in sends(0):
            send.start()

    for i in range(3, len(groups)):
        for load in loads(i):
            load.start()

    @pl.when(c < n_ctx - 1)
    def _():
        for send in to_right:
            send.start()

    @pl.when(c > 0)
    def _():
        for send in to_left:
            send.start()

    @pl.when(c == 0)
    def _():
        u_left[...] = jnp.zeros_like(u_left)

    @pl.when(c == n_ctx - 1)
    def _():
        q_right[...] = jnp.zeros_like(q_right)
        g_right[...] = jnp.zeros_like(g_right)

    for i in range(1, len(groups)):
        for load in loads(i):
            load.wait()
        interior(i)
        if i < early:

            @pl.when(jnp.logical_not(first))
            def _():
                for send in sends(i):
                    send.start()

    @pl.when(c > 0)
    def _():
        for send in to_right:
            send.wait_recv()

    @pl.when(c < n_ctx - 1)
    def _():
        for send in to_left:
            send.wait_recv()

    dh[...] = jnp.zeros_like(dh)
    lax.fori_loop(0, width // LANES, edges, 0)

    @pl.when(jnp.logical_not(first))
    def _():
        for send in edge_sends():
            send.start()

    shares = []
    for d in range(1, n_ctx):
        other = lax.rem(c + d, n_ctx)
        shares.append(
            pltpu.make_async_remote_copy(
                src_ref=dh.at[:, pl.ds(pl.multiple_of(other * own, own), own)], dst_ref=dh_in.at[d - 1],
                send_sem=dh_send.at[d - 1], recv_sem=dh_recv.at[d - 1],
                device_id={"ctx": other}, device_id_type=MESH,
            )
        )
    for share in shares:
        share.start()
    for share in shares:
        share.wait_recv()
    mine = dh[:, pl.ds(pl.multiple_of(c * own, own), own)]
    for d in range(1, n_ctx):
        mine = mine + dh_in[d - 1]
    half = own // 2
    total[...] = jnp.concatenate([mine[:, :half], mine[:, half:]], axis=0).astype(jnp.bfloat16)
    swap = pltpu.make_async_remote_copy(
        src_ref=total, dst_ref=mirrored, send_sem=mirror_send, recv_sem=mirror_recv,
        device_id={"pipe": mirror}, device_id_type=MESH,
    )
    swap.start()

    @pl.when(jnp.logical_not(first))
    def _():
        for i in range(early, len(groups)):
            for send in sends(i):
                send.start()

    @pl.when(last)
    def _():
        arrived[...] = jnp.zeros_like(arrived)

    swap.wait_recv()
    theirs = mirrored[...].astype(jnp.float32)
    for j in range(taps):
        summed[j, :, :half] = mine[j : j + 1, :half] + theirs[j : j + 1]
        summed[j, :, half:] = mine[j : j + 1, half:] + theirs[8 + j : 9 + j]
    swap.wait_send()
    for share in shares:
        share.wait_send()

    @pl.when(c < n_ctx - 1)
    def _():
        for send in to_right:
            send.wait_send()

    @pl.when(c > 0)
    def _():
        for send in to_left:
            send.wait_send()

    @pl.when(jnp.logical_not(first))
    def _():
        for i in range(len(groups)):
            for send in sends(i):
                send.wait_send()
        for send in edge_sends():
            send.wait_send()

    @pl.when(jnp.logical_not(last))
    def _():
        for i in range(len(groups)):
            for send in sends(i):
                send.wait_recv()
        for send in edge_sends():
            send.wait_recv()


def finish(arrived, summed, passed, grad, sem, grad_sem):
    rows = arrived.shape[2]
    part = rows // PARTS
    copies = [pltpu.make_async_copy(summed, grad, grad_sem)]
    for k in range(2):
        for i in range(PARTS):
            at = pl.ds(i * part, part)
            copies.append(pltpu.make_async_copy(arrived.at[k, 0, at], passed.at[k, 0, at], sem.at[k, i]))
    for copy in copies:
        copy.start()
    for copy in copies:
        copy.wait()


def local(n_pipe, n_ctx, query, inner, out_grad, filters, trace_lengths):
    _, rows, width = query.shape
    taps = filters.shape[1]
    own = width // n_ctx
    groups = len(groups_of(width))
    vmem = pl.BlockSpec(memory_space=pltpu.VMEM)
    operands = (trace_lengths, query[0], inner[0], out_grad[0], jnp.swapaxes(filters, 0, 1))
    f32, bf16, dma = jnp.float32, jnp.bfloat16, pltpu.SemaphoreType.DMA
    arrived, summed = pl.pallas_call(
        functools.partial(kernel, n_pipe, n_ctx, trace_lengths.shape[1]),
        out_shape=(pltpu.VMEM((2, 1, rows, width), bf16), pltpu.VMEM((taps, 1, own), f32)),
        in_specs=[pl.BlockSpec(memory_space=pltpu.HBM)] * 5,
        out_specs=(vmem, vmem),
        scratch_shapes=[
            pltpu.SMEM(trace_lengths.shape, jnp.int32),
            pltpu.VMEM((rows, width), bf16),
            pltpu.VMEM((rows, width), bf16),
            pltpu.VMEM((rows, width), bf16),
            pltpu.VMEM((taps, 1, width), f32),
            pltpu.VMEM((EDGE, width), bf16),
            pltpu.VMEM((EDGE, width), bf16),
            pltpu.VMEM((EDGE, width), bf16),
            pltpu.VMEM((rows + EDGE, LANES), f32),
            pltpu.VMEM((rows + EDGE, LANES), f32),
            pltpu.VMEM((taps - 1, rows + EDGE, LANES), f32),
            pltpu.VMEM((taps, EDGE // 2, width), f32),
            pltpu.VMEM((2, rows, width), bf16),
            pltpu.VMEM((8, width), f32),
            pltpu.VMEM((n_ctx - 1, 8, own), f32),
            pltpu.VMEM((16, own // 2), bf16),
            pltpu.VMEM((16, own // 2), bf16),
            dma,
            dma((3, groups)),
            dma,
            dma((3,)),
            dma((3,)),
            dma((2, groups)),
            dma((2, groups)),
            dma((2,)),
            dma((2,)),
            dma((n_ctx - 1,)),
            dma((n_ctx - 1,)),
            dma,
            dma,
        ],
        compiler_params=pltpu.CompilerParams(collective_id=0, has_side_effects=True, vmem_limit_bytes=48 * 1024 * 1024),
        name="grads_passed_on",
    )(*(pltpu.with_memory_space_constraint(x, pltpu.HBM) for x in operands))
    passed, grad = pl.pallas_call(
        finish,
        out_shape=(jax.ShapeDtypeStruct((2, 1, rows, width), bf16), jax.ShapeDtypeStruct((taps, 1, own), f32)),
        in_specs=[pl.BlockSpec(memory_space=pl.ANY)] * 2,
        out_specs=(pl.BlockSpec(memory_space=pl.ANY),) * 2,
        scratch_shapes=[dma((2, PARTS)), dma],
        compiler_params=pltpu.CompilerParams(vmem_limit_bytes=1024 * 1024),
        name="results_written",
    )(*(pltpu.with_memory_space_constraint(x, pltpu.VMEM) for x in (arrived, summed)))
    return passed, jnp.swapaxes(grad, 0, 1)


def solution(mesh):
    in_specs = (
        P("pipe", "ctx", None),
        P("pipe", "ctx", None),
        P("pipe", "ctx", None),
        P("pipe", None, None),
        P("pipe", None),
    )
    out_specs = (P(None, "pipe", "ctx", None), P("pipe", None, "ctx"))
    run = functools.partial(local, mesh.shape["pipe"], mesh.shape["ctx"])
    return jax.shard_map(run, mesh=mesh, in_specs=in_specs, out_specs=out_specs, check_vma=False)
```

```python
import functools

import jax
import jax.numpy as jnp
from jax import lax
from jax.experimental import pallas as pl
from jax.experimental.pallas import tpu as pltpu
from jax.sharding import PartitionSpec as P

MESH = pl.DeviceIdType.MESH
EDGE = 16
LANES = 128
PARTS = 4
FIRST_GROUPS = (128, 128, 256, 512, 1024)
GROUP = 2048


def groups_of(width):
    sizes = list(FIRST_GROUPS)
    while sum(sizes) < width:
        sizes.append(min(GROUP, width - sum(sizes)))
    return [(sum(sizes[:i]), size) for i, size in enumerate(sizes)]


def fold(x):
    return x[: EDGE // 2] + x[EDGE // 2 :]


def rounded_product(a, b):
    return (a.astype(jnp.float32) * b.astype(jnp.float32)).astype(jnp.bfloat16).astype(jnp.float32)


def kernel(
    n_pipe, n_ctx, n_seg,
    trace_lengths, query, inner, out_grad, filters, arrived, summed,
    lengths, q_v, u_v, g_v, f_v, u_left, q_right, g_right, u_f, gz_f, masks, parts, staged, dh, dh_in, total, mirrored,
    length_sem, load_sem, filter_sem, halo_send, halo_recv, out_send, out_recv, edge_send, edge_recv, dh_send, dh_recv, mirror_send, mirror_recv,
):
    taps, _, width = filters.shape
    rows = query.shape[0]
    own = width // n_ctx
    groups = groups_of(width)
    early = sum(start < width // 2 for start, _ in groups)
    s = lax.axis_index("pipe")
    c = lax.axis_index("ctx")
    first, last = s == 0, s == n_pipe - 1
    before, after = lax.rem(s + n_pipe - 1, n_pipe), lax.rem(s + 1, n_pipe)
    mirror = n_pipe - 1 - s

    def cols_of(i):
        return pl.ds(*groups[i])

    def loads(i):
        cols = cols_of(i)
        return [
            pltpu.make_async_copy(src.at[:, cols], dst.at[:, cols], load_sem.at[k, i])
            for k, (src, dst) in enumerate(((query, q_v), (inner, u_v), (out_grad, g_v)))
        ]

    head = pl.ds(0, LANES)
    rest = pl.ds(LANES, width - LANES)
    filter_loads = [
        pltpu.make_async_copy(filters.at[:, :, cols], f_v.at[:, :, cols], filter_sem.at[k])
        for k, cols in enumerate((head, rest))
    ]
    length_load = pltpu.make_async_copy(trace_lengths, lengths, length_sem)
    length_load.start()
    for load in loads(0):
        load.start()
    filter_loads[0].start()

    barrier = pltpu.get_barrier_semaphore()
    for other in (before, after, mirror):
        pl.semaphore_signal(barrier, inc=1, device_id={"pipe": other}, device_id_type=MESH)
    for d in range(1, n_ctx):
        pl.semaphore_signal(barrier, inc=1, device_id={"ctx": lax.rem(c + d, n_ctx)}, device_id_type=MESH)

    filter_loads[1].start()
    for i in range(1, 4):
        for load in loads(i):
            load.start()


    length_load.wait()
    ends = []
    for k in range(n_seg):
        ends.append(lengths[0, k] + (ends[-1] if ends else 0))
    pos = c * rows + lax.broadcasted_iota(jnp.int32, (rows + EDGE, LANES), 0)

    def seg_of(at):
        return sum((at >= end).astype(jnp.int32) for end in ends)

    seg = seg_of(pos)
    for j in range(1, taps):
        masks[j - 1] = (seg == seg_of(pos - j)).astype(jnp.float32)

    def back(j, base, mask_at):
        x = u_f[base - j : base - j + EDGE]
        return x if j == 0 else x * masks[j - 1, mask_at : mask_at + EDGE]

    def ahead(j, base, mask_at):
        x = gz_f[base + j : base + j + EDGE]
        return x if j == 0 else x * masks[j - 1, mask_at + j : mask_at + j + EDGE]

    def taps_at(cols):
        return [jnp.broadcast_to(f_v[j, :, cols], (EDGE, LANES)) for j in range(taps)]

    def interior(i):
        def group(l, carry):
            cols = pl.ds(pl.multiple_of(groups[i][0] + l * LANES, LANES), LANES)
            u_f[EDGE : EDGE + rows] = u_v[:, cols].astype(jnp.float32)
            gz_f[:rows] = rounded_product(g_v[:, cols], q_v[:, cols])
            f = taps_at(cols)
            sums = [jnp.zeros((EDGE // 2, LANES), jnp.float32)] * taps
            for at in range(0, rows, EDGE):
                if at > 0:
                    gz = gz_f[at : at + EDGE]
                    z = None
                    for j in range(taps):
                        u = back(j, EDGE + at, at)
                        z = f[j] * u if z is None else z + f[j] * u
                        sums[j] = sums[j] + fold(gz * u)
                    staged[0, at : at + EDGE, cols] = (g_v[at : at + EDGE, cols].astype(jnp.float32) * z).astype(jnp.bfloat16)
                if at < rows - EDGE:
                    z = f[0] * ahead(0, at, at)
                    for j in range(1, taps):
                        z = z + f[j] * ahead(j, at, at)
                    staged[1, at : at + EDGE, cols] = z.astype(jnp.bfloat16)
            for j in range(taps):
                parts[j, :, cols] = sums[j]
            return carry

        lax.fori_loop(0, groups[i][1] // LANES, group, 0)

    def edges(l, carry):
        cols = pl.ds(pl.multiple_of(l * LANES, LANES), LANES)
        f = taps_at(cols)
        u_f[:EDGE] = u_left[:, cols].astype(jnp.float32)
        u_f[EDGE : 2 * EDGE] = u_v[:EDGE, cols].astype(jnp.float32)
        gz_f[:EDGE] = rounded_product(g_v[rows - EDGE :, cols], q_v[rows - EDGE :, cols])
        gz_f[EDGE : 2 * EDGE] = rounded_product(g_right[:, cols], q_right[:, cols])
        gz = rounded_product(g_v[:EDGE, cols], q_v[:EDGE, cols])
        z = None
        for j in range(taps):
            u = back(j, EDGE, 0)
            z = f[j] * u if z is None else z + f[j] * u
            dh[j : j + 1, cols] = jnp.sum(parts[j, :, cols] + fold(gz * u), axis=0, keepdims=True)
        staged[0, :EDGE, cols] = (g_v[:EDGE, cols].astype(jnp.float32) * z).astype(jnp.bfloat16)
        z = f[0] * ahead(0, 0, rows - EDGE)
        for j in range(1, taps):
            z = z + f[j] * ahead(j, 0, rows - EDGE)
        staged[1, rows - EDGE :, cols] = z.astype(jnp.bfloat16)
        return carry

    def sends(i):
        cols = cols_of(i)
        return [
            pltpu.make_async_remote_copy(
                src_ref=staged.at[k, at, cols], dst_ref=arrived.at[k, 0, at, cols],
                send_sem=out_send.at[k, i], recv_sem=out_recv.at[k, i],
                device_id={"pipe": before}, device_id_type=MESH,
            )
            for k, at in enumerate((pl.ds(EDGE, rows - EDGE), pl.ds(0, rows - EDGE)))
        ]

    def edge_sends():
        return [
            pltpu.make_async_remote_copy(
                src_ref=staged.at[k, at], dst_ref=arrived.at[k, 0, at],
                send_sem=edge_send.at[k], recv_sem=edge_recv.at[k],
                device_id={"pipe": before}, device_id_type=MESH,
            )
            for k, at in enumerate((pl.ds(0, EDGE), pl.ds(rows - EDGE, EDGE)))
        ]

    def halo(k, src, dst, other):
        return pltpu.make_async_remote_copy(
            src_ref=src, dst_ref=dst, send_sem=halo_send.at[k], recv_sem=halo_recv.at[k],
            device_id={"ctx": other}, device_id_type=MESH,
        )

    to_right = [halo(0, inner.at[pl.ds(rows - EDGE, EDGE)], u_left, lax.rem(c + 1, n_ctx))]
    to_left = [
        halo(1, query.at[pl.ds(0, EDGE)], q_right, lax.rem(c + n_ctx - 1, n_ctx)),
        halo(2, out_grad.at[pl.ds(0, EDGE)], g_right, lax.rem(c + n_ctx - 1, n_ctx)),
    ]

    filter_loads[0].wait()
    for load in loads(0):
        load.wait()
    interior(0)
    pl.semaphore_wait(barrier, 3 + n_ctx - 1)

    @pl.when(jnp.logical_not(first))
    def _():
        for send in sends(0):
            send.start()

    for i in range(4, len(groups)):
        for load in loads(i):
            load.start()

    @pl.when(c < n_ctx - 1)
    def _():
        for send in to_right:
            send.start()

    @pl.when(c > 0)
    def _():
        for send in to_left:
            send.start()

    @pl.when(c == 0)
    def _():
        u_left[...] = jnp.zeros_like(u_left)

    @pl.when(c == n_ctx - 1)
    def _():
        q_right[...] = jnp.zeros_like(q_right)
        g_right[...] = jnp.zeros_like(g_right)

    filter_loads[1].wait()
    for i in range(1, len(groups)):
        for load in loads(i):
            load.wait()
        interior(i)
        if i < early:

            @pl.when(jnp.logical_not(first))
            def _():
                for send in sends(i):
                    send.start()

    @pl.when(c > 0)
    def _():
        for send in to_right:
            send.wait_recv()

    @pl.when(c < n_ctx - 1)
    def _():
        for send in to_left:
            send.wait_recv()

    dh[...] = jnp.zeros_like(dh)
    lax.fori_loop(0, width // LANES, edges, 0)

    @pl.when(jnp.logical_not(first))
    def _():
        for send in edge_sends():
            send.start()

    shares = []
    for d in range(1, n_ctx):
        other = lax.rem(c + d, n_ctx)
        shares.append(
            pltpu.make_async_remote_copy(
                src_ref=dh.at[:, pl.ds(pl.multiple_of(other * own, own), own)], dst_ref=dh_in.at[d - 1],
                send_sem=dh_send.at[d - 1], recv_sem=dh_recv.at[d - 1],
                device_id={"ctx": other}, device_id_type=MESH,
            )
        )
    for share in shares:
        share.start()
    for share in shares:
        share.wait_recv()
    mine = dh[:, pl.ds(pl.multiple_of(c * own, own), own)]
    for d in range(1, n_ctx):
        mine = mine + dh_in[d - 1]
    half = own // 2
    total[...] = jnp.concatenate([mine[:, :half], mine[:, half:]], axis=0).astype(jnp.bfloat16)
    swap = pltpu.make_async_remote_copy(
        src_ref=total, dst_ref=mirrored, send_sem=mirror_send, recv_sem=mirror_recv,
        device_id={"pipe": mirror}, device_id_type=MESH,
    )
    swap.start()

    @pl.when(jnp.logical_not(first))
    def _():
        for i in range(early, len(groups)):
            for send in sends(i):
                send.start()

    @pl.when(last)
    def _():
        arrived[...] = jnp.zeros_like(arrived)

    swap.wait_recv()
    theirs = mirrored[...].astype(jnp.float32)
    for j in range(taps):
        summed[j, :, :half] = mine[j : j + 1, :half] + theirs[j : j + 1]
        summed[j, :, half:] = mine[j : j + 1, half:] + theirs[8 + j : 9 + j]
    swap.wait_send()
    for share in shares:
        share.wait_send()

    @pl.when(c < n_ctx - 1)
    def _():
        for send in to_right:
            send.wait_send()

    @pl.when(c > 0)
    def _():
        for send in to_left:
            send.wait_send()

    @pl.when(jnp.logical_not(first))
    def _():
        for i in range(len(groups)):
            for send in sends(i):
                send.wait_send()
        for send in edge_sends():
            send.wait_send()

    @pl.when(jnp.logical_not(last))
    def _():
        for i in range(len(groups)):
            for send in sends(i):
                send.wait_recv()
        for send in edge_sends():
            send.wait_recv()


def finish(arrived, summed, passed, grad, sem, grad_sem):
    rows = arrived.shape[2]
    part = rows // PARTS
    copies = [pltpu.make_async_copy(summed, grad, grad_sem)]
    for k in range(2):
        for i in range(PARTS):
            at = pl.ds(i * part, part)
            copies.append(pltpu.make_async_copy(arrived.at[k, 0, at], passed.at[k, 0, at], sem.at[k, i]))
    for copy in copies:
        copy.start()
    for copy in copies:
        copy.wait()


def local(n_pipe, n_ctx, query, inner, out_grad, filters, trace_lengths):
    _, rows, width = query.shape
    taps = filters.shape[1]
    own = width // n_ctx
    groups = len(groups_of(width))
    vmem = pl.BlockSpec(memory_space=pltpu.VMEM)
    operands = (trace_lengths, query[0], inner[0], out_grad[0], jnp.swapaxes(filters, 0, 1))
    f32, bf16, dma = jnp.float32, jnp.bfloat16, pltpu.SemaphoreType.DMA
    arrived, summed = pl.pallas_call(
        functools.partial(kernel, n_pipe, n_ctx, trace_lengths.shape[1]),
        out_shape=(pltpu.VMEM((2, 1, rows, width), bf16), pltpu.VMEM((taps, 1, own), f32)),
        in_specs=[pl.BlockSpec(memory_space=pltpu.HBM)] * 5,
        out_specs=(vmem, vmem),
        scratch_shapes=[
            pltpu.SMEM(trace_lengths.shape, jnp.int32),
            pltpu.VMEM((rows, width), bf16),
            pltpu.VMEM((rows, width), bf16),
            pltpu.VMEM((rows, width), bf16),
            pltpu.VMEM((taps, 1, width), f32),
            pltpu.VMEM((EDGE, width), bf16),
            pltpu.VMEM((EDGE, width), bf16),
            pltpu.VMEM((EDGE, width), bf16),
            pltpu.VMEM((rows + EDGE, LANES), f32),
            pltpu.VMEM((rows + EDGE, LANES), f32),
            pltpu.VMEM((taps - 1, rows + EDGE, LANES), f32),
            pltpu.VMEM((taps, EDGE // 2, width), f32),
            pltpu.VMEM((2, rows, width), bf16),
            pltpu.VMEM((8, width), f32),
            pltpu.VMEM((n_ctx - 1, 8, own), f32),
            pltpu.VMEM((16, own // 2), bf16),
            pltpu.VMEM((16, own // 2), bf16),
            dma,
            dma((3, groups)),
            dma((2,)),
            dma((3,)),
            dma((3,)),
            dma((2, groups)),
            dma((2, groups)),
            dma((2,)),
            dma((2,)),
            dma((n_ctx - 1,)),
            dma((n_ctx - 1,)),
            dma,
            dma,
        ],
        compiler_params=pltpu.CompilerParams(collective_id=0, has_side_effects=True, vmem_limit_bytes=48 * 1024 * 1024),
        name="grads_passed_on",
    )(*(pltpu.with_memory_space_constraint(x, pltpu.HBM) for x in operands))
    passed, grad = pl.pallas_call(
        finish,
        out_shape=(jax.ShapeDtypeStruct((2, 1, rows, width), bf16), jax.ShapeDtypeStruct((taps, 1, own), f32)),
        in_specs=[pl.BlockSpec(memory_space=pl.ANY)] * 2,
        out_specs=(pl.BlockSpec(memory_space=pl.ANY),) * 2,
        scratch_shapes=[dma((2, PARTS)), dma],
        compiler_params=pltpu.CompilerParams(vmem_limit_bytes=1024 * 1024),
        name="results_written",
    )(*(pltpu.with_memory_space_constraint(x, pltpu.VMEM) for x in (arrived, summed)))
    return passed, jnp.swapaxes(grad, 0, 1)


def solution(mesh):
    in_specs = (
        P("pipe", "ctx", None),
        P("pipe", "ctx", None),
        P("pipe", "ctx", None),
        P("pipe", None, None),
        P("pipe", None),
    )
    out_specs = (P(None, "pipe", "ctx", None), P("pipe", None, "ctx"))
    run = functools.partial(local, mesh.shape["pipe"], mesh.shape["ctx"])
    return jax.shard_map(run, mesh=mesh, in_specs=in_specs, out_specs=out_specs, check_vma=False)
```

```python
import functools

import jax
import jax.numpy as jnp
from jax import lax
from jax.experimental import pallas as pl
from jax.experimental.pallas import tpu as pltpu
from jax.sharding import PartitionSpec as P

MESH = pl.DeviceIdType.MESH
EDGE = 16
LANES = 128
PARTS = 4
FIRST_GROUPS = (128, 128, 256, 512, 1024)
GROUP = 2048


def groups_of(width):
    sizes = list(FIRST_GROUPS)
    while sum(sizes) < width:
        sizes.append(min(GROUP, width - sum(sizes)))
    return [(sum(sizes[:i]), size) for i, size in enumerate(sizes)]


def fold(x):
    return x[: EDGE // 2] + x[EDGE // 2 :]


def rounded_product(a, b):
    return (a.astype(jnp.float32) * b.astype(jnp.float32)).astype(jnp.bfloat16).astype(jnp.float32)


def kernel(
    n_pipe, n_ctx, n_seg,
    trace_lengths, query, inner, out_grad, filters, arrived, summed,
    lengths, q_v, u_v, g_v, f_v, u_left, q_right, g_right, u_f, gz_f, masks, parts, staged, dh, dh_in, total, mirrored,
    length_sem, load_sem, filter_sem, halo_send, halo_recv, out_send, out_recv, edge_send, edge_recv, dh_send, dh_recv, mirror_send, mirror_recv,
):
    taps, _, width = filters.shape
    rows = query.shape[0]
    own = width // n_ctx
    groups = groups_of(width)
    early = sum(start < width // 2 for start, _ in groups)
    s = lax.axis_index("pipe")
    c = lax.axis_index("ctx")
    first, last = s == 0, s == n_pipe - 1
    before, after = lax.rem(s + n_pipe - 1, n_pipe), lax.rem(s + 1, n_pipe)
    mirror = n_pipe - 1 - s

    def cols_of(i):
        return pl.ds(*groups[i])

    def loads(i):
        cols = cols_of(i)
        return [
            pltpu.make_async_copy(src.at[:, cols], dst.at[:, cols], load_sem.at[k, i])
            for k, (src, dst) in enumerate(((query, q_v), (inner, u_v), (out_grad, g_v)))
        ]

    head = pl.ds(0, LANES)
    rest = pl.ds(LANES, width - LANES)
    filter_loads = [
        pltpu.make_async_copy(filters.at[:, :, cols], f_v.at[:, :, cols], filter_sem.at[k])
        for k, cols in enumerate((head, rest))
    ]
    length_load = pltpu.make_async_copy(trace_lengths, lengths, length_sem)
    length_load.start()
    for load in loads(0):
        load.start()
    filter_loads[0].start()

    barrier = pltpu.get_barrier_semaphore()
    for other in (before, after, mirror):
        pl.semaphore_signal(barrier, inc=1, device_id={"pipe": other}, device_id_type=MESH)
    for d in range(1, n_ctx):
        pl.semaphore_signal(barrier, inc=1, device_id={"ctx": lax.rem(c + d, n_ctx)}, device_id_type=MESH)

    filter_loads[1].start()
    for i in range(1, 4):
        for load in loads(i):
            load.start()


    length_load.wait()
    ends = []
    for k in range(n_seg):
        ends.append(lengths[0, k] + (ends[-1] if ends else 0))
    pos = c * rows + lax.broadcasted_iota(jnp.int32, (rows + EDGE, LANES), 0)

    def seg_of(at):
        return sum((at >= end).astype(jnp.int32) for end in ends)

    seg = seg_of(pos)
    for j in range(1, taps):
        masks[j - 1] = (seg == seg_of(pos - j)).astype(jnp.float32)

    def back(j, base, mask_at):
        x = u_f[base - j : base - j + EDGE]
        return x if j == 0 else x * masks[j - 1, mask_at : mask_at + EDGE]

    def ahead(j, base, mask_at):
        x = gz_f[base + j : base + j + EDGE]
        return x if j == 0 else x * masks[j - 1, mask_at + j : mask_at + j + EDGE]

    def taps_at(cols):
        return [jnp.broadcast_to(f_v[j, :, cols], (EDGE, LANES)) for j in range(taps)]

    def interior(i):
        def group(l, carry):
            cols = pl.ds(pl.multiple_of(groups[i][0] + l * LANES, LANES), LANES)
            u_f[EDGE : EDGE + rows] = u_v[:, cols].astype(jnp.float32)
            gz_f[:rows] = rounded_product(g_v[:, cols], q_v[:, cols])
            f = taps_at(cols)
            sums = [jnp.zeros((EDGE // 2, LANES), jnp.float32)] * taps
            for at in range(0, rows, EDGE):
                if at > 0:
                    gz = gz_f[at : at + EDGE]
                    z = None
                    for j in range(taps):
                        u = back(j, EDGE + at, at)
                        z = f[j] * u if z is None else z + f[j] * u
                        sums[j] = sums[j] + fold(gz * u)
                    staged[0, at : at + EDGE, cols] = (g_v[at : at + EDGE, cols].astype(jnp.float32) * z).astype(jnp.bfloat16)
                if at < rows - EDGE:
                    z = f[0] * ahead(0, at, at)
                    for j in range(1, taps):
                        z = z + f[j] * ahead(j, at, at)
                    staged[1, at : at + EDGE, cols] = z.astype(jnp.bfloat16)
            for j in range(taps):
                parts[j, :, cols] = sums[j]
            return carry

        lax.fori_loop(0, groups[i][1] // LANES, group, 0)

    def edges(l, carry):
        cols = pl.ds(pl.multiple_of(l * LANES, LANES), LANES)
        f = taps_at(cols)
        u_f[:EDGE] = u_left[:, cols].astype(jnp.float32)
        u_f[EDGE : 2 * EDGE] = u_v[:EDGE, cols].astype(jnp.float32)
        gz_f[:EDGE] = rounded_product(g_v[rows - EDGE :, cols], q_v[rows - EDGE :, cols])
        gz_f[EDGE : 2 * EDGE] = rounded_product(g_right[:, cols], q_right[:, cols])
        gz = rounded_product(g_v[:EDGE, cols], q_v[:EDGE, cols])
        z = None
        for j in range(taps):
            u = back(j, EDGE, 0)
            z = f[j] * u if z is None else z + f[j] * u
            dh[j : j + 1, cols] = jnp.sum(parts[j, :, cols] + fold(gz * u), axis=0, keepdims=True)
        staged[0, :EDGE, cols] = (g_v[:EDGE, cols].astype(jnp.float32) * z).astype(jnp.bfloat16)
        z = f[0] * ahead(0, 0, rows - EDGE)
        for j in range(1, taps):
            z = z + f[j] * ahead(j, 0, rows - EDGE)
        staged[1, rows - EDGE :, cols] = z.astype(jnp.bfloat16)
        return carry

    def sends(i):
        cols = cols_of(i)
        return [
            pltpu.make_async_remote_copy(
                src_ref=staged.at[k, at, cols], dst_ref=arrived.at[k, 0, at, cols],
                send_sem=out_send.at[k, i], recv_sem=out_recv.at[k, i],
                device_id={"pipe": before}, device_id_type=MESH,
            )
            for k, at in enumerate((pl.ds(EDGE, rows - EDGE), pl.ds(0, rows - EDGE)))
        ]

    def edge_sends():
        return [
            pltpu.make_async_remote_copy(
                src_ref=staged.at[k, at], dst_ref=arrived.at[k, 0, at],
                send_sem=edge_send.at[k], recv_sem=edge_recv.at[k],
                device_id={"pipe": before}, device_id_type=MESH,
            )
            for k, at in enumerate((pl.ds(0, EDGE), pl.ds(rows - EDGE, EDGE)))
        ]

    def halo(k, src, dst, other):
        return pltpu.make_async_remote_copy(
            src_ref=src, dst_ref=dst, send_sem=halo_send.at[k], recv_sem=halo_recv.at[k],
            device_id={"ctx": other}, device_id_type=MESH,
        )

    to_right = [halo(0, inner.at[pl.ds(rows - EDGE, EDGE)], u_left, lax.rem(c + 1, n_ctx))]
    to_left = [
        halo(1, query.at[pl.ds(0, EDGE)], q_right, lax.rem(c + n_ctx - 1, n_ctx)),
        halo(2, out_grad.at[pl.ds(0, EDGE)], g_right, lax.rem(c + n_ctx - 1, n_ctx)),
    ]

    filter_loads[0].wait()
    for load in loads(0):
        load.wait()
    interior(0)
    pl.semaphore_wait(barrier, 3 + n_ctx - 1)

    @pl.when(jnp.logical_not(first))
    def _():
        for send in sends(0):
            send.start()

    for i in range(4, len(groups)):
        for load in loads(i):
            load.start()

    @pl.when(c < n_ctx - 1)
    def _():
        for send in to_right:
            send.start()

    @pl.when(c > 0)
    def _():
        for send in to_left:
            send.start()

    @pl.when(c == 0)
    def _():
        u_left[...] = jnp.zeros_like(u_left)

    @pl.when(c == n_ctx - 1)
    def _():
        q_right[...] = jnp.zeros_like(q_right)
        g_right[...] = jnp.zeros_like(g_right)

    filter_loads[1].wait()
    for i in range(1, len(groups)):
        for load in loads(i):
            load.wait()
        interior(i)
        if i < early:

            @pl.when(jnp.logical_not(first))
            def _():
                for send in sends(i):
                    send.start()

    @pl.when(c > 0)
    def _():
        for send in to_right:
            send.wait_recv()

    @pl.when(c < n_ctx - 1)
    def _():
        for send in to_left:
            send.wait_recv()

    dh[...] = jnp.zeros_like(dh)
    lax.fori_loop(0, width // LANES, edges, 0)

    @pl.when(jnp.logical_not(first))
    def _():
        for send in edge_sends():
            send.start()

    shares = []
    for d in range(1, n_ctx):
        other = lax.rem(c + d, n_ctx)
        shares.append(
            pltpu.make_async_remote_copy(
                src_ref=dh.at[:, pl.ds(pl.multiple_of(other * own, own), own)], dst_ref=dh_in.at[d - 1],
                send_sem=dh_send.at[d - 1], recv_sem=dh_recv.at[d - 1],
                device_id={"ctx": other}, device_id_type=MESH,
            )
        )
    for share in shares:
        share.start()
    for share in shares:
        share.wait_recv()
    mine = dh[:, pl.ds(pl.multiple_of(c * own, own), own)]
    for d in range(1, n_ctx):
        mine = mine + dh_in[d - 1]
    half = own // 2
    total[...] = jnp.concatenate([mine[:, :half], mine[:, half:]], axis=0).astype(jnp.bfloat16)
    swap = pltpu.make_async_remote_copy(
        src_ref=total, dst_ref=mirrored, send_sem=mirror_send, recv_sem=mirror_recv,
        device_id={"pipe": mirror}, device_id_type=MESH,
    )
    swap.start()

    @pl.when(jnp.logical_not(first))
    def _():
        for i in range(early, len(groups)):
            for send in sends(i):
                send.start()

    @pl.when(last)
    def _():
        arrived[...] = jnp.zeros_like(arrived)

    swap.wait_recv()
    theirs = mirrored[...].astype(jnp.float32)
    for j in range(taps):
        summed[j, :, :half] = mine[j : j + 1, :half] + theirs[j : j + 1]
        summed[j, :, half:] = mine[j : j + 1, half:] + theirs[8 + j : 9 + j]
    swap.wait_send()
    for share in shares:
        share.wait_send()

    @pl.when(c < n_ctx - 1)
    def _():
        for send in to_right:
            send.wait_send()

    @pl.when(c > 0)
    def _():
        for send in to_left:
            send.wait_send()

    @pl.when(jnp.logical_not(first))
    def _():
        for i in range(len(groups)):
            for send in sends(i):
                send.wait_send()
        for send in edge_sends():
            send.wait_send()

    @pl.when(jnp.logical_not(last))
    def _():
        for i in range(len(groups)):
            for send in sends(i):
                send.wait_recv()
        for send in edge_sends():
            send.wait_recv()


def finish(arrived, summed, passed, grad, sem, grad_sem):
    rows = arrived.shape[2]
    part = rows // PARTS
    copies = [pltpu.make_async_copy(summed, grad, grad_sem)]
    for k in range(2):
        for i in range(PARTS):
            at = pl.ds(i * part, part)
            copies.append(pltpu.make_async_copy(arrived.at[k, 0, at], passed.at[k, 0, at], sem.at[k, i]))
    for i, copy in enumerate(copies):
        copy.start(priority=i % 2)
    for copy in copies:
        copy.wait()


def local(n_pipe, n_ctx, query, inner, out_grad, filters, trace_lengths):
    _, rows, width = query.shape
    taps = filters.shape[1]
    own = width // n_ctx
    groups = len(groups_of(width))
    vmem = pl.BlockSpec(memory_space=pltpu.VMEM)
    operands = (trace_lengths, query[0], inner[0], out_grad[0], jnp.swapaxes(filters, 0, 1))
    f32, bf16, dma = jnp.float32, jnp.bfloat16, pltpu.SemaphoreType.DMA
    arrived, summed = pl.pallas_call(
        functools.partial(kernel, n_pipe, n_ctx, trace_lengths.shape[1]),
        out_shape=(pltpu.VMEM((2, 1, rows, width), bf16), pltpu.VMEM((taps, 1, own), f32)),
        in_specs=[pl.BlockSpec(memory_space=pltpu.HBM)] * 5,
        out_specs=(vmem, vmem),
        scratch_shapes=[
            pltpu.SMEM(trace_lengths.shape, jnp.int32),
            pltpu.VMEM((rows, width), bf16),
            pltpu.VMEM((rows, width), bf16),
            pltpu.VMEM((rows, width), bf16),
            pltpu.VMEM((taps, 1, width), f32),
            pltpu.VMEM((EDGE, width), bf16),
            pltpu.VMEM((EDGE, width), bf16),
            pltpu.VMEM((EDGE, width), bf16),
            pltpu.VMEM((rows + EDGE, LANES), f32),
            pltpu.VMEM((rows + EDGE, LANES), f32),
            pltpu.VMEM((taps - 1, rows + EDGE, LANES), f32),
            pltpu.VMEM((taps, EDGE // 2, width), f32),
            pltpu.VMEM((2, rows, width), bf16),
            pltpu.VMEM((8, width), f32),
            pltpu.VMEM((n_ctx - 1, 8, own), f32),
            pltpu.VMEM((16, own // 2), bf16),
            pltpu.VMEM((16, own // 2), bf16),
            dma,
            dma((3, groups)),
            dma((2,)),
            dma((3,)),
            dma((3,)),
            dma((2, groups)),
            dma((2, groups)),
            dma((2,)),
            dma((2,)),
            dma((n_ctx - 1,)),
            dma((n_ctx - 1,)),
            dma,
            dma,
        ],
        compiler_params=pltpu.CompilerParams(collective_id=0, has_side_effects=True, vmem_limit_bytes=48 * 1024 * 1024),
        name="grads_passed_on",
    )(*(pltpu.with_memory_space_constraint(x, pltpu.HBM) for x in operands))
    passed, grad = pl.pallas_call(
        finish,
        out_shape=(jax.ShapeDtypeStruct((2, 1, rows, width), bf16), jax.ShapeDtypeStruct((taps, 1, own), f32)),
        in_specs=[pl.BlockSpec(memory_space=pl.ANY)] * 2,
        out_specs=(pl.BlockSpec(memory_space=pl.ANY),) * 2,
        scratch_shapes=[dma((2, PARTS)), dma],
        compiler_params=pltpu.CompilerParams(vmem_limit_bytes=1024 * 1024),
        name="results_written",
    )(*(pltpu.with_memory_space_constraint(x, pltpu.VMEM) for x in (arrived, summed)))
    return passed, jnp.swapaxes(grad, 0, 1)


def solution(mesh):
    in_specs = (
        P("pipe", "ctx", None),
        P("pipe", "ctx", None),
        P("pipe", "ctx", None),
        P("pipe", None, None),
        P("pipe", None),
    )
    out_specs = (P(None, "pipe", "ctx", None), P("pipe", None, "ctx"))
    run = functools.partial(local, mesh.shape["pipe"], mesh.shape["ctx"])
    return jax.shard_map(run, mesh=mesh, in_specs=in_specs, out_specs=out_specs, check_vma=False)
```

```python
import functools

import jax
import jax.numpy as jnp
from jax import lax
from jax.experimental import pallas as pl
from jax.experimental.pallas import tpu as pltpu
from jax.sharding import PartitionSpec as P

MESH = pl.DeviceIdType.MESH
EDGE = 16
LANES = 128
PARTS = 4
FIRST_GROUPS = (256, 256, 512, 1024)
GROUP = 2048


def groups_of(width):
    sizes = list(FIRST_GROUPS)
    while sum(sizes) < width:
        sizes.append(min(GROUP, width - sum(sizes)))
    return [(sum(sizes[:i]), size) for i, size in enumerate(sizes)]


def fold(x):
    return x[: EDGE // 2] + x[EDGE // 2 :]


def rounded_product(a, b):
    return (a.astype(jnp.float32) * b.astype(jnp.float32)).astype(jnp.bfloat16).astype(jnp.float32)


def kernel(
    n_pipe, n_ctx, n_seg,
    trace_lengths, query, inner, out_grad, filters, arrived, summed,
    lengths, q_v, u_v, g_v, f_v, u_left, q_right, g_right, u_f, gz_f, masks, parts, staged, dh, dh_in, total, mirrored,
    length_sem, load_sem, filter_sem, halo_send, halo_recv, out_send, out_recv, edge_send, edge_recv, dh_send, dh_recv, mirror_send, mirror_recv,
):
    taps, _, width = filters.shape
    rows = query.shape[0]
    own = width // n_ctx
    groups = groups_of(width)
    early = sum(start < width * 3 // 4 for start, _ in groups)
    s = lax.axis_index("pipe")
    c = lax.axis_index("ctx")
    first, last = s == 0, s == n_pipe - 1
    before, after = lax.rem(s + n_pipe - 1, n_pipe), lax.rem(s + 1, n_pipe)
    mirror = n_pipe - 1 - s

    def cols_of(i):
        return pl.ds(*groups[i])

    def loads(i):
        cols = cols_of(i)
        return [
            pltpu.make_async_copy(src.at[:, cols], dst.at[:, cols], load_sem.at[k, i])
            for k, (src, dst) in enumerate(((query, q_v), (inner, u_v), (out_grad, g_v)))
        ]

    length_load = pltpu.make_async_copy(trace_lengths, lengths, length_sem)
    length_load.start()
    filter_load = pltpu.make_async_copy(filters, f_v, filter_sem)
    filter_load.start()
    for i in range(3):
        for load in loads(i):
            load.start()

    barrier = pltpu.get_barrier_semaphore()
    for other in (before, after, mirror):
        pl.semaphore_signal(barrier, inc=1, device_id={"pipe": other}, device_id_type=MESH)
    for d in range(1, n_ctx):
        pl.semaphore_signal(barrier, inc=1, device_id={"ctx": lax.rem(c + d, n_ctx)}, device_id_type=MESH)

    length_load.wait()
    ends = []
    for k in range(n_seg):
        ends.append(lengths[0, k] + (ends[-1] if ends else 0))
    pos = c * rows + lax.broadcasted_iota(jnp.int32, (rows + EDGE, LANES), 0)

    def seg_of(at):
        return sum((at >= end).astype(jnp.int32) for end in ends)

    seg = seg_of(pos)
    for j in range(1, taps):
        masks[j - 1] = (seg == seg_of(pos - j)).astype(jnp.float32)

    def back(j, base, mask_at):
        x = u_f[base - j : base - j + EDGE]
        return x if j == 0 else x * masks[j - 1, mask_at : mask_at + EDGE]

    def ahead(j, base, mask_at):
        x = gz_f[base + j : base + j + EDGE]
        return x if j == 0 else x * masks[j - 1, mask_at + j : mask_at + j + EDGE]

    def taps_at(cols):
        return [jnp.broadcast_to(f_v[j, :, cols], (EDGE, LANES)) for j in range(taps)]

    def interior(i):
        def group(l, carry):
            cols = pl.ds(pl.multiple_of(groups[i][0] + l * LANES, LANES), LANES)
            u_f[EDGE : EDGE + rows] = u_v[:, cols].astype(jnp.float32)
            gz_f[:rows] = rounded_product(g_v[:, cols], q_v[:, cols])
            f = taps_at(cols)
            sums = [jnp.zeros((EDGE // 2, LANES), jnp.float32)] * taps
            for at in range(0, rows, EDGE):
                if at > 0:
                    gz = gz_f[at : at + EDGE]
                    z = None
                    for j in range(taps):
                        u = back(j, EDGE + at, at)
                        z = f[j] * u if z is None else z + f[j] * u
                        sums[j] = sums[j] + fold(gz * u)
                    staged[0, at : at + EDGE, cols] = (g_v[at : at + EDGE, cols].astype(jnp.float32) * z).astype(jnp.bfloat16)
                if at < rows - EDGE:
                    z = f[0] * ahead(0, at, at)
                    for j in range(1, taps):
                        z = z + f[j] * ahead(j, at, at)
                    staged[1, at : at + EDGE, cols] = z.astype(jnp.bfloat16)
            for j in range(taps):
                parts[j, :, cols] = sums[j]
            return carry

        lax.fori_loop(0, groups[i][1] // LANES, group, 0)

    def edges(l, carry):
        cols = pl.ds(pl.multiple_of(l * LANES, LANES), LANES)
        f = taps_at(cols)
        u_f[:EDGE] = u_left[:, cols].astype(jnp.float32)
        u_f[EDGE : 2 * EDGE] = u_v[:EDGE, cols].astype(jnp.float32)
        gz_f[:EDGE] = rounded_product(g_v[rows - EDGE :, cols], q_v[rows - EDGE :, cols])
        gz_f[EDGE : 2 * EDGE] = rounded_product(g_right[:, cols], q_right[:, cols])
        gz = rounded_product(g_v[:EDGE, cols], q_v[:EDGE, cols])
        z = None
        for j in range(taps):
            u = back(j, EDGE, 0)
            z = f[j] * u if z is None else z + f[j] * u
            dh[j : j + 1, cols] = jnp.sum(parts[j, :, cols] + fold(gz * u), axis=0, keepdims=True)
        staged[0, :EDGE, cols] = (g_v[:EDGE, cols].astype(jnp.float32) * z).astype(jnp.bfloat16)
        z = f[0] * ahead(0, 0, rows - EDGE)
        for j in range(1, taps):
            z = z + f[j] * ahead(j, 0, rows - EDGE)
        staged[1, rows - EDGE :, cols] = z.astype(jnp.bfloat16)
        return carry

    def sends(i):
        cols = cols_of(i)
        return [
            pltpu.make_async_remote_copy(
                src_ref=staged.at[k, at, cols], dst_ref=arrived.at[k, 0, at, cols],
                send_sem=out_send.at[k, i], recv_sem=out_recv.at[k, i],
                device_id={"pipe": before}, device_id_type=MESH,
            )
            for k, at in enumerate((pl.ds(EDGE, rows - EDGE), pl.ds(0, rows - EDGE)))
        ]

    def edge_sends():
        return [
            pltpu.make_async_remote_copy(
                src_ref=staged.at[k, at], dst_ref=arrived.at[k, 0, at],
                send_sem=edge_send.at[k], recv_sem=edge_recv.at[k],
                device_id={"pipe": before}, device_id_type=MESH,
            )
            for k, at in enumerate((pl.ds(0, EDGE), pl.ds(rows - EDGE, EDGE)))
        ]

    def halo(k, src, dst, other):
        return pltpu.make_async_remote_copy(
            src_ref=src, dst_ref=dst, send_sem=halo_send.at[k], recv_sem=halo_recv.at[k],
            device_id={"ctx": other}, device_id_type=MESH,
        )

    to_right = [halo(0, inner.at[pl.ds(rows - EDGE, EDGE)], u_left, lax.rem(c + 1, n_ctx))]
    to_left = [
        halo(1, query.at[pl.ds(0, EDGE)], q_right, lax.rem(c + n_ctx - 1, n_ctx)),
        halo(2, out_grad.at[pl.ds(0, EDGE)], g_right, lax.rem(c + n_ctx - 1, n_ctx)),
    ]

    filter_load.wait()
    for load in loads(0):
        load.wait()
    interior(0)
    pl.semaphore_wait(barrier, 3 + n_ctx - 1)

    @pl.when(jnp.logical_not(first))
    def _():
        for send in sends(0):
            send.start()

    for i in range(3, len(groups)):
        for load in loads(i):
            load.start()

    @pl.when(c < n_ctx - 1)
    def _():
        for send in to_right:
            send.start()

    @pl.when(c > 0)
    def _():
        for send in to_left:
            send.start()

    @pl.when(c == 0)
    def _():
        u_left[...] = jnp.zeros_like(u_left)

    @pl.when(c == n_ctx - 1)
    def _():
        q_right[...] = jnp.zeros_like(q_right)
        g_right[...] = jnp.zeros_like(g_right)

    for i in range(1, len(groups)):
        for load in loads(i):
            load.wait()
        interior(i)
        if i < early:

            @pl.when(jnp.logical_not(first))
            def _():
                for send in sends(i):
                    send.start()

    @pl.when(c > 0)
    def _():
        for send in to_right:
            send.wait_recv()

    @pl.when(c < n_ctx - 1)
    def _():
        for send in to_left:
            send.wait_recv()

    dh[...] = jnp.zeros_like(dh)
    lax.fori_loop(0, width // LANES, edges, 0)

    @pl.when(jnp.logical_not(first))
    def _():
        for send in edge_sends():
            send.start()

    shares = []
    for d in range(1, n_ctx):
        other = lax.rem(c + d, n_ctx)
        shares.append(
            pltpu.make_async_remote_copy(
                src_ref=dh.at[:, pl.ds(pl.multiple_of(other * own, own), own)], dst_ref=dh_in.at[d - 1],
                send_sem=dh_send.at[d - 1], recv_sem=dh_recv.at[d - 1],
                device_id={"ctx": other}, device_id_type=MESH,
            )
        )
    for share in shares:
        share.start()
    for share in shares:
        share.wait_recv()
    mine = dh[:, pl.ds(pl.multiple_of(c * own, own), own)]
    for d in range(1, n_ctx):
        mine = mine + dh_in[d - 1]
    half = own // 2
    total[...] = jnp.concatenate([mine[:, :half], mine[:, half:]], axis=0).astype(jnp.bfloat16)
    swap = pltpu.make_async_remote_copy(
        src_ref=total, dst_ref=mirrored, send_sem=mirror_send, recv_sem=mirror_recv,
        device_id={"pipe": mirror}, device_id_type=MESH,
    )
    swap.start()

    @pl.when(jnp.logical_not(first))
    def _():
        for i in range(early, len(groups)):
            for send in sends(i):
                send.start()

    @pl.when(last)
    def _():
        arrived[...] = jnp.zeros_like(arrived)

    swap.wait_recv()
    theirs = mirrored[...].astype(jnp.float32)
    for j in range(taps):
        summed[j, :, :half] = mine[j : j + 1, :half] + theirs[j : j + 1]
        summed[j, :, half:] = mine[j : j + 1, half:] + theirs[8 + j : 9 + j]
    swap.wait_send()
    for share in shares:
        share.wait_send()

    @pl.when(c < n_ctx - 1)
    def _():
        for send in to_right:
            send.wait_send()

    @pl.when(c > 0)
    def _():
        for send in to_left:
            send.wait_send()

    @pl.when(jnp.logical_not(first))
    def _():
        for i in range(len(groups)):
            for send in sends(i):
                send.wait_send()
        for send in edge_sends():
            send.wait_send()

    @pl.when(jnp.logical_not(last))
    def _():
        for i in range(len(groups)):
            for send in sends(i):
                send.wait_recv()
        for send in edge_sends():
            send.wait_recv()


def finish(arrived, summed, passed, grad, sem, grad_sem):
    rows = arrived.shape[2]
    part = rows // PARTS
    copies = [pltpu.make_async_copy(summed, grad, grad_sem)]
    for k in range(2):
        for i in range(PARTS):
            at = pl.ds(i * part, part)
            copies.append(pltpu.make_async_copy(arrived.at[k, 0, at], passed.at[k, 0, at], sem.at[k, i]))
    for copy in copies:
        copy.start()
    for copy in copies:
        copy.wait()


def local(n_pipe, n_ctx, query, inner, out_grad, filters, trace_lengths):
    _, rows, width = query.shape
    taps = filters.shape[1]
    own = width // n_ctx
    groups = len(groups_of(width))
    vmem = pl.BlockSpec(memory_space=pltpu.VMEM)
    operands = (trace_lengths, query[0], inner[0], out_grad[0], jnp.swapaxes(filters, 0, 1))
    f32, bf16, dma = jnp.float32, jnp.bfloat16, pltpu.SemaphoreType.DMA
    arrived, summed = pl.pallas_call(
        functools.partial(kernel, n_pipe, n_ctx, trace_lengths.shape[1]),
        out_shape=(pltpu.VMEM((2, 1, rows, width), bf16), pltpu.VMEM((taps, 1, own), f32)),
        in_specs=[pl.BlockSpec(memory_space=pltpu.HBM)] * 5,
        out_specs=(vmem, vmem),
        scratch_shapes=[
            pltpu.SMEM(trace_lengths.shape, jnp.int32),
            pltpu.VMEM((rows, width), bf16),
            pltpu.VMEM((rows, width), bf16),
            pltpu.VMEM((rows, width), bf16),
            pltpu.VMEM((taps, 1, width), f32),
            pltpu.VMEM((EDGE, width), bf16),
            pltpu.VMEM((EDGE, width), bf16),
            pltpu.VMEM((EDGE, width), bf16),
            pltpu.VMEM((rows + EDGE, LANES), f32),
            pltpu.VMEM((rows + EDGE, LANES), f32),
            pltpu.VMEM((taps - 1, rows + EDGE, LANES), f32),
            pltpu.VMEM((taps, EDGE // 2, width), f32),
            pltpu.VMEM((2, rows, width), bf16),
            pltpu.VMEM((8, width), f32),
            pltpu.VMEM((n_ctx - 1, 8, own), f32),
            pltpu.VMEM((16, own // 2), bf16),
            pltpu.VMEM((16, own // 2), bf16),
            dma,
            dma((3, groups)),
            dma,
            dma((3,)),
            dma((3,)),
            dma((2, groups)),
            dma((2, groups)),
            dma((2,)),
            dma((2,)),
            dma((n_ctx - 1,)),
            dma((n_ctx - 1,)),
            dma,
            dma,
        ],
        compiler_params=pltpu.CompilerParams(collective_id=0, has_side_effects=True, vmem_limit_bytes=48 * 1024 * 1024),
        name="grads_passed_on",
    )(*(pltpu.with_memory_space_constraint(x, pltpu.HBM) for x in operands))
    passed, grad = pl.pallas_call(
        finish,
        out_shape=(jax.ShapeDtypeStruct((2, 1, rows, width), bf16), jax.ShapeDtypeStruct((taps, 1, own), f32)),
        in_specs=[pl.BlockSpec(memory_space=pl.ANY)] * 2,
        out_specs=(pl.BlockSpec(memory_space=pl.ANY),) * 2,
        scratch_shapes=[dma((2, PARTS)), dma],
        compiler_params=pltpu.CompilerParams(vmem_limit_bytes=1024 * 1024),
        name="results_written",
    )(*(pltpu.with_memory_space_constraint(x, pltpu.VMEM) for x in (arrived, summed)))
    return passed, jnp.swapaxes(grad, 0, 1)


def solution(mesh):
    in_specs = (
        P("pipe", "ctx", None),
        P("pipe", "ctx", None),
        P("pipe", "ctx", None),
        P("pipe", None, None),
        P("pipe", None),
    )
    out_specs = (P(None, "pipe", "ctx", None), P("pipe", None, "ctx"))
    run = functools.partial(local, mesh.shape["pipe"], mesh.shape["ctx"])
    return jax.shard_map(run, mesh=mesh, in_specs=in_specs, out_specs=out_specs, check_vma=False)
```
